32 devices in a mesh: island: 2 (over y), fsdp: 16 (over z, x, core).
Axes of the slice: x: 2, y: 2, z: 4, core: 2. Of those that a mesh axis runs over, the one named last changes fastest.
Arguments:
- momentum: float32 [2, 32768, 128], P('island', 'fsdp'), may hold values from -6 to 6
- gradient: bfloat16 [2, 32768, 128], P('island', 'fsdp'), may hold values from -6 to 6
- params: float32 [32768, 128], P('fsdp'), may hold values from -6 to 6
- indices: int32 [2, 32768, 32], P('island', 'fsdp'), may hold values from 0 to 127, all different within a row
Outputs:
- new_momentum: float32 [2, 32768, 128], P('island', 'fsdp')
- new_params: bfloat16 [32768, 128], P('fsdp')
The draws below stay inside these ranges and needn't reach their ends.
Inputs may be any that keep to these rules, and one draw needn't show every extreme that they name: `indices`: the 32 numbers of one island and block are distinct.
All inputs are finite; a program needn't handle non-finite values.
Results may differ from the reference program's by a relative error of at most 0.001.
Values may be sent and summed in bfloat16 or wider, within the bound.
No kernel may reach another device: no remote copies, remote signals or barrier semaphores. Data moves between devices by JAX's collectives and lax.ppermute only.
A program may use at most 64 MiB of HBM per device.

```python
import jax
import jax.numpy as jnp
from jax import lax

BLOCK = 128
KEEP = 32
BLOCKS = 32768
N_ISLAND = 2


def shard_levels(rng, shape, split, low, top_value):
    loudness = 1.0
    for dim, shards_of in split:
        draws = jax.random.uniform(jax.random.fold_in(jax.random.fold_in(rng, 6), dim), (shards_of,), jnp.float32, low / len(split), top_value / len(split))
        loudness = loudness * jnp.repeat(jnp.exp(draws), shape[dim] // shards_of).reshape((-1,) + (1,) * (len(shape) - 1 - dim))
    return loudness


def different_ones(own_key, rows, count, top, lift):
    ranking = jax.random.permutation(jax.random.fold_in(own_key, 1), count)
    boost = ranking
    for power in range(3):
        boost = boost * boost // count
    boost = boost * lift // count
    lots = jax.random.randint(jax.random.fold_in(own_key, 2), (rows, count), 0, 4096) + boost
    sure = jax.random.permutation(jax.random.fold_in(own_key, 3), rows)[jnp.arange(count) % rows]
    lots = jnp.where(jnp.arange(rows)[:, None] == sure[None, :], 1 << 14, lots)
    merit = lots * count + jnp.arange(count)
    return lax.top_k(merit.astype(jnp.int32), top)[1].astype(jnp.int32)


def scatter_about(key, extent, width, reach, pieces=(), held_as=jnp.bfloat16):
    entries = width * jax.random.normal(key, extent, jnp.float32)
    if pieces:
        entries = entries * shard_levels(key, extent, pieces, -0.22, 0.18)
    return jnp.clip(entries, -reach, reach).astype(held_as)


def setup_inputs(seed: int = 0) -> dict:
    arg_keys = jax.random.split(jax.random.key(seed), 5)
    momentum = scatter_about(arg_keys[0], (N_ISLAND, BLOCKS, BLOCK), 1.0, 6.0, ((0, 2), (1, 16)), jnp.float32)
    gradient = scatter_about(arg_keys[1], (N_ISLAND, BLOCKS, BLOCK), 1.0, 6.0, ((0, 2), (1, 16)))
    params = scatter_about(arg_keys[2], (BLOCKS, BLOCK), 1.0, 6.0, ((0, 16),), jnp.float32)
    indices = different_ones(arg_keys[3], N_ISLAND * BLOCKS, BLOCK, KEEP, 0).reshape((N_ISLAND, BLOCKS, KEEP))
    return {"momentum": momentum, "gradient": gradient, "params": params, "indices": indices}


def dct_table(length):
    freq = jnp.arange(length, dtype=jnp.float32)[:, None]
    place = jnp.arange(length, dtype=jnp.float32)[None, :]
    scale = jnp.where(freq == 0, jnp.sqrt(1.0 / length), jnp.sqrt(2.0 / length))
    return scale * jnp.cos(jnp.pi * (place + 0.5) * freq / length)

def reference(momentum, gradient, params, indices):
    table = dct_table(BLOCK)
    mom = 0.999 * momentum + gradient.astype(jnp.float32)
    coef = jnp.einsum('ics,ts->ict', mom, table, precision=lax.Precision.HIGHEST)
    counter = jnp.arange(BLOCK, dtype=jnp.int32)
    mask = jnp.zeros(coef.shape, jnp.float32)
    for slot in range(KEEP):
        mask = mask + (indices[:, :, slot:slot + 1] == counter).astype(jnp.float32)
    kept = coef * mask
    new_momentum = mom - jnp.einsum('ict,ts->ics', kept, table, precision=lax.Precision.HIGHEST)
    total = lax.optimization_barrier(jnp.sum(kept, axis=0))
    update = jnp.dot(total / N_ISLAND, table, precision=lax.Precision.HIGHEST, preferred_element_type=jnp.float32)
    new_params = (params - update).astype(jnp.bfloat16)
    return (new_momentum, new_params)
```

```python
import functools

import jax
import jax.numpy as jnp
import numpy as np
from jax import lax
from jax.experimental import pallas as pl
from jax.experimental.pallas import tpu as pltpu
from jax.sharding import PartitionSpec as P

STEPS = 32000.0
GROUPS = 4
TINY = 1e-30


def dct_weights(length):
    freq = np.arange(length, dtype=np.float64)[:, None]
    place = np.arange(length, dtype=np.float64)[None, :]
    scale = np.where(freq == 0, np.sqrt(1.0 / length), np.sqrt(2.0 / length))
    table = scale * np.cos(np.pi * (place + 0.5) * freq / length)

    def pair(a):
        hi = a.astype(jnp.bfloat16)
        lo = (a - hi.astype(np.float64)).astype(jnp.bfloat16)
        return np.block([[hi, lo], [hi, np.zeros_like(hi)]]).astype(jnp.bfloat16)

    return pair(table.T), pair(table)


def transform(x, weights):
    hi = x.astype(jnp.bfloat16)
    lo = (x - hi.astype(jnp.float32)).astype(jnp.bfloat16)
    both = jnp.dot(
        jnp.concatenate([hi, lo], axis=1), weights, preferred_element_type=jnp.float32
    )
    length = x.shape[1]
    return both[:, :length] + both[:, length:]


def lanes_of(x, index):
    return jnp.take_along_axis(x, index, axis=1, mode="promise_in_bounds")


def stack_groups(numbers, length):
    return jnp.concatenate(
        [numbers[:, g * length : (g + 1) * length] for g in range(GROUPS)], axis=0
    )


def encode_kernel(w_ref, idx_ref, m_ref, g_ref, msg_ref, scale_ref):
    step = pl.program_id(0)
    length = m_ref.shape[1]
    keep = idx_ref.shape[0]
    mom = 0.999 * m_ref[...] + g_ref[...].astype(jnp.float32)
    coef = transform(mom, w_ref[...])
    picks = stack_groups(idx_ref[...], length).T
    group = lax.broadcasted_iota(jnp.int32, (length, length), 1) // keep
    values = lanes_of(coef[:length], picks)
    for g in range(1, GROUPS):
        values = jnp.where(group == g, lanes_of(coef[g * length : (g + 1) * length], picks), values)
    turned = values.T
    coded = []
    for g in range(GROUPS):
        part = turned[g * keep : (g + 1) * keep]
        top = jnp.max(jnp.abs(part), axis=0, keepdims=True)
        power = jnp.ceil(jnp.log2(jnp.maximum(top, TINY)))
        scale_ref[pl.ds(step * GROUPS + g, 1), :] = power
        coded.append(jnp.round(part * (STEPS * jnp.exp2(-power))))
    rows = pl.ds(pl.multiple_of(step * length, length), length)
    msg_ref[rows, :] = jnp.concatenate(coded, axis=0).astype(jnp.int32).astype(jnp.int16)

    @pl.when(step == pl.num_programs(0) - 1)
    def _():
        tail = scale_ref.shape[0]
        msg_ref[pl.ds(msg_ref.shape[0] - tail, tail), :] = (
            scale_ref[...].astype(jnp.int32).astype(jnp.int16)
        )


def positions(numbers, length):
    keep, blocks = numbers.shape
    out = []
    for b in range(blocks // length):
        part = numbers[:, b * length : (b + 1) * length]
        place = lax.broadcasted_iota(jnp.int32, (length, length), 0)
        found = jnp.full((length, length), -1, jnp.int32)
        for k in range(keep):
            found = jnp.where(part[k : k + 1] == place, (b % GROUPS) * keep + k, found)
        out.append(found.T)
    return jnp.concatenate(out, axis=0)


def decode(coded, powers, keep):
    values = coded.astype(jnp.int32).astype(jnp.float32)
    unit = jnp.exp2(powers) * (1.0 / STEPS)
    parts = [values[g * keep : (g + 1) * keep] * unit[g : g + 1] for g in range(GROUPS)]
    return jnp.concatenate(parts, axis=0).T


def spread(values, lanes):
    length = values.shape[0]
    out = []
    for g in range(GROUPS):
        at = lanes[g * length : (g + 1) * length]
        out.append(jnp.where(at >= 0, lanes_of(values, at & (length - 1)), 0.0))
    return jnp.concatenate(out, axis=0)


def message_part(msg_ref, step, length, keep):
    rows = pl.ds(pl.multiple_of(step * length, length), length)
    tail = scale_rows(msg_ref.shape[0] * length // keep, length)
    base = msg_ref.shape[0] - tail
    powers = msg_ref[pl.ds(base, tail), :].astype(jnp.int32).astype(jnp.float32)
    mine = []
    row = lax.broadcasted_iota(jnp.int32, powers.shape, 0)
    for g in range(GROUPS):
        mine.append(
            jnp.sum(jnp.where(row == step * GROUPS + g, powers, 0.0), axis=0, keepdims=True)
        )
    return msg_ref[rows, :], jnp.concatenate(mine, axis=0)


def own_kernel(w_ref, idx_ref, msg_ref, m_ref, g_ref, new_ref, back_ref):
    step = pl.program_id(0)
    length = m_ref.shape[1]
    keep = idx_ref.shape[0]
    coded, powers = message_part(msg_ref, step, length, keep)
    kept = spread(decode(coded, powers, keep), positions(idx_ref[...], length))
    back = transform(kept, w_ref[...])
    back_ref[...] = back
    new_ref[...] = 0.999 * m_ref[...] + g_ref[...].astype(jnp.float32) - back


def positions_kernel(idx_ref, lanes_ref):
    length = lanes_ref.shape[1]
    lanes_ref[...] = positions(idx_ref[...].astype(jnp.int32), length)


def finish_kernel(islands, me_ref, w_ref, back_ref, p_ref, *refs):
    out_ref = refs[-1]
    msgs, lanes = refs[: islands - 1], refs[islands - 1 : 2 * islands - 2]
    step = pl.program_id(0)
    length = p_ref.shape[1]
    keep = length // GROUPS
    terms = [back_ref[...]]
    for msg_ref, lanes_ref in zip(msgs, lanes):
        coded, powers = message_part(msg_ref, step, length, keep)
        kept = spread(decode(coded, powers, keep), lanes_ref[...])
        terms.append(transform(kept, w_ref[...]))
    if islands == 2:
        total = terms[0] + terms[1]
    else:
        total = None
        for island in range(islands):
            term = terms[0]
            for away in range(1, islands):
                origin = lax.rem(me_ref[0] + islands - away, islands)
                term = jnp.where(origin == island, terms[away], term)
            total = term if total is None else total + term
    out_ref[...] = (p_ref[...] - total * (1.0 / islands)).astype(out_ref.dtype)


def scale_rows(blocks, length):
    return -(-(blocks // length) // 16) * 16


def local(momentum, gradient, params, indices):
    islands = lax.axis_size("island")
    _, count, length = momentum.shape
    keep = indices.shape[2]
    chunk = GROUPS * length
    grid = (count // chunk,)
    forward, inverse = (jnp.asarray(w) for w in dct_weights(length))
    numbers = indices[0].T
    short = numbers.astype(jnp.int16)
    rings = [
        [(i, (i + away) % islands) for i in range(islands)] for away in range(1, islands)
    ]
    other_numbers = [lax.ppermute(short, "island", ring) for ring in rings]

    tail = scale_rows(count, length)
    msg_rows = count * keep // length + tail
    weights_spec = pl.BlockSpec((2 * length, 2 * length), lambda i: (0, 0))
    numbers_spec = pl.BlockSpec((keep, chunk), lambda i: (0, i))
    rows_spec = pl.BlockSpec((chunk, length), lambda i: (i, 0))
    msg_spec = pl.BlockSpec((msg_rows, length), lambda i: (0, 0))
    wide = jax.ShapeDtypeStruct((count, length), jnp.float32)

    msg = pl.pallas_call(
        encode_kernel,
        grid=grid,
        in_specs=[weights_spec, numbers_spec, rows_spec, rows_spec],
        out_specs=msg_spec,
        out_shape=jax.ShapeDtypeStruct((msg_rows, length), jnp.int16),
        scratch_shapes=[pltpu.VMEM((tail, length), jnp.float32)],
        name="encode",
    )(forward, numbers, momentum[0], gradient[0])
    other_msgs = [lax.ppermute(msg, "island", ring) for ring in rings]

    new_momentum, back = pl.pallas_call(
        own_kernel,
        grid=grid,
        in_specs=[weights_spec, numbers_spec, msg_spec, rows_spec, rows_spec],
        out_specs=(rows_spec, rows_spec),
        out_shape=(wide, wide),
        cost_estimate=pl.CostEstimate(flops=10**9, bytes_accessed=6 * 2**20, transcendentals=0),
        name="own",
    )(inverse, numbers, msg, momentum[0], gradient[0])

    lanes = [
        pl.pallas_call(
            positions_kernel,
            grid=grid,
            in_specs=[numbers_spec],
            out_specs=rows_spec,
            out_shape=jax.ShapeDtypeStruct((count, length), jnp.int32),
            cost_estimate=pl.CostEstimate(flops=10**9, bytes_accessed=2 * 2**20, transcendentals=0),
            name="positions",
        )(other)
        for other in other_numbers
    ]

    me = lax.axis_index("island").astype(jnp.int32)[None]
    new_params = pl.pallas_call(
        functools.partial(finish_kernel, islands),
        grid=grid,
        in_specs=[pl.BlockSpec(memory_space=pltpu.SMEM), weights_spec, rows_spec, rows_spec]
        + [msg_spec] * (islands - 1)
        + [rows_spec] * (islands - 1),
        out_specs=rows_spec,
        out_shape=jax.ShapeDtypeStruct((count, length), jnp.bfloat16),
        name="finish",
    )(me, inverse, back, params, *other_msgs, *lanes)
    return new_momentum[None], new_params


def solution(mesh):
    in_specs = (
        P("island", "fsdp", None),
        P("island", "fsdp", None),
        P("fsdp", None),
        P("island", "fsdp", None),
    )
    out_specs = (P("island", "fsdp", None), P("fsdp", None))
    return jax.shard_map(local, mesh=mesh, in_specs=in_specs, out_specs=out_specs, check_vma=False)
```

```python
import functools

import jax
import jax.numpy as jnp
import numpy as np
from jax import lax
from jax.experimental import pallas as pl
from jax.experimental.pallas import tpu as pltpu
from jax.sharding import PartitionSpec as P

STEPS = 32000.0
GROUPS = 4
TINY = 1e-30
WORD = 32
SUB = 8
VMEM_LIMIT = 16 * 2**20


def dct_table(length):
    freq = np.arange(length, dtype=np.float64)[:, None]
    place = np.arange(length, dtype=np.float64)[None, :]
    scale = np.where(freq == 0, np.sqrt(1.0 / length), np.sqrt(2.0 / length))
    return (scale * np.cos(np.pi * (place + 0.5) * freq / length)).astype(np.float32)


def two_parts(x):
    hi = x.astype(jnp.bfloat16)
    return hi, (x - hi.astype(jnp.float32)).astype(jnp.bfloat16)


def weights_of(table):
    hi, lo = two_parts(table)
    return jnp.concatenate(
        [jnp.concatenate([hi, lo], axis=1), jnp.concatenate([hi, jnp.zeros_like(hi)], axis=1)],
        axis=0,
    )


def transform(x, weights):
    both = jnp.dot(
        jnp.concatenate(two_parts(x), axis=1), weights, preferred_element_type=jnp.float32
    )
    length = x.shape[1]
    return both[:, :length] + both[:, length:]


def lanes_of(x, index):
    return jnp.take_along_axis(x, index, axis=1, mode="promise_in_bounds")


def row_iota():
    return lax.broadcasted_iota(jnp.int32, (SUB, 128), 0)


def mask_words(part, length):
    rows = [part[v : v + SUB] for v in range(0, part.shape[0], SUB)]
    bits = [lax.shift_left(jnp.ones_like(r), r & (WORD - 1)) for r in rows]
    words = []
    for w in range(length // WORD):
        total = None
        for r, bit in zip(rows, bits):
            term = jnp.where(lax.shift_right_logical(r, 5) == w, bit, 0)
            total = term if total is None else total + term
        for shift in (4, 2, 1):
            total = total + pltpu.roll(total, shift, 0)
        words.append(total)
    return words


def bases_of(words):
    bases = [jnp.zeros_like(words[0])]
    for word in words[:-1]:
        bases.append(bases[-1] + lax.population_count(word))
    return bases


def sorted_numbers(part, length):
    words = mask_words(part, length)
    bases = bases_of(words)
    out = []
    for v in range(0, part.shape[0], SUB):
        rank = row_iota() + v
        word, base, place = words[0], bases[0], jnp.zeros_like(rank)
        for w in range(1, len(words)):
            up = rank >= bases[w]
            word = jnp.where(up, words[w], word)
            base = jnp.where(up, bases[w], base)
            place = jnp.where(up, w * WORD, place)
        rank = rank - base
        half = WORD // 2
        while half:
            below = lax.population_count(word & ((1 << half) - 1))
            up = rank >= below
            rank = jnp.where(up, rank - below, rank)
            word = jnp.where(up, lax.shift_right_logical(word, half), word)
            place = jnp.where(up, place + half, place)
            half //= 2
        out.append(place)
    return jnp.concatenate(out, axis=0)


def positions(part, group, length):
    keep = part.shape[0]
    words = mask_words(part, length)
    bases = bases_of(words)
    out = []
    for t in range(0, length, SUB):
        place = row_iota() + t % WORD
        word = words[t // WORD]
        low = lax.shift_left(jnp.ones_like(place), place) - 1
        rank = lax.population_count(word & low) + (bases[t // WORD] + group * keep)
        held = lax.shift_right_logical(word, place) & 1
        out.append(jnp.where(held == 1, rank, -1))
    return jnp.concatenate(out, axis=0).T


def all_positions(numbers, length):
    return [
        positions(numbers[:, b * length : (b + 1) * length], b % GROUPS, length)
        for b in range(numbers.shape[1] // length)
    ]


def encode_kernel(table_ref, idx_ref, m_ref, g_ref, msg_ref):
    count, length = m_ref.shape
    keep = idx_ref.shape[0]
    weights = weights_of(table_ref[...].T)
    group = lax.broadcasted_iota(jnp.int32, (length, length), 1) // keep
    scales = []
    for c in range(count // (GROUPS * length)):
        picks = jnp.concatenate(
            [
                sorted_numbers(idx_ref[:, b * length : (b + 1) * length], length)
                for b in range(c * GROUPS, (c + 1) * GROUPS)
            ],
            axis=0,
        ).T
        rows = slice(c * GROUPS * length, (c + 1) * GROUPS * length)
        mom = 0.999 * m_ref[rows] + g_ref[rows].astype(jnp.float32)
        coef = transform(mom, weights)
        values = lanes_of(coef[:length], picks)
        for g in range(1, GROUPS):
            other = lanes_of(coef[g * length : (g + 1) * length], picks)
            values = jnp.where(group == g, other, values)
        turned = values.T
        coded = []
        for g in range(GROUPS):
            part = turned[g * keep : (g + 1) * keep]
            top = jnp.max(jnp.abs(part), axis=0, keepdims=True)
            power = jnp.ceil(jnp.log2(jnp.maximum(top, TINY)))
            scales.append(power)
            coded.append(jnp.round(part * (STEPS * jnp.exp2(-power))))
        msg_ref[c * length : (c + 1) * length] = (
            jnp.concatenate(coded, axis=0).astype(jnp.int32).astype(jnp.int16)
        )
    rows = msg_ref.shape[0] - count * keep // length
    if rows > len(scales):
        scales.append(jnp.zeros((rows - len(scales), length), jnp.float32))
    msg_ref[msg_ref.shape[0] - rows :] = (
        jnp.concatenate(scales, axis=0).astype(jnp.int32).astype(jnp.int16)
    )


def spread(msg_ref, lanes, c, keep):
    length = msg_ref.shape[1]
    rows = msg_ref[c * length : (c + 1) * length].astype(jnp.int32).astype(jnp.float32)
    chunks = msg_ref.shape[0] // length
    tail = msg_ref[chunks * length :].astype(jnp.int32).astype(jnp.float32)
    unit = jnp.exp2(tail[c * GROUPS : (c + 1) * GROUPS]) * (1.0 / STEPS)
    values = jnp.concatenate(
        [rows[g * keep : (g + 1) * keep] * unit[g : g + 1] for g in range(GROUPS)], axis=0
    ).T
    return jnp.concatenate(
        [jnp.where(at >= 0, lanes_of(values, at & (length - 1)), 0.0) for at in lanes], axis=0
    )


def own_kernel(table_ref, idx_ref, msg_ref, m_ref, g_ref, new_ref, back_ref):
    count, length = m_ref.shape
    keep = idx_ref.shape[0]
    weights = weights_of(table_ref[...])
    for c in range(count // (GROUPS * length)):
        rows = slice(c * GROUPS * length, (c + 1) * GROUPS * length)
        lanes = all_positions(idx_ref[:, rows], length)
        back = transform(spread(msg_ref, lanes, c, keep), weights)
        back_ref[rows] = back
        new_ref[rows] = 0.999 * m_ref[rows] + g_ref[rows].astype(jnp.float32) - back


def positions_kernel(idx_ref, lanes_ref):
    length = lanes_ref.shape[1]
    numbers = idx_ref[...].astype(jnp.int32)
    for b, lanes in enumerate(all_positions(numbers, length)):
        lanes_ref[b * length : (b + 1) * length] = lanes


def finish_kernel(islands, me_ref, table_ref, back_ref, p_ref, *refs):
    out_ref = refs[-1]
    msgs, places = refs[: islands - 1], refs[islands - 1 : 2 * islands - 2]
    count, length = p_ref.shape
    keep = length // GROUPS
    weights = weights_of(table_ref[...])
    for c in range(count // (GROUPS * length)):
        rows = slice(c * GROUPS * length, (c + 1) * GROUPS * length)
        terms = [back_ref[rows]]
        for msg_ref, lanes_ref in zip(msgs, places):
            lanes = [
                lanes_ref[b * length : (b + 1) * length]
                for b in range(c * GROUPS, (c + 1) * GROUPS)
            ]
            terms.append(transform(spread(msg_ref, lanes, c, keep), weights))
        if islands == 2:
            total = terms[0] + terms[1]
        else:
            total = None
            for island in range(islands):
                term = terms[0]
                for away in range(1, islands):
                    origin = lax.rem(me_ref[0] + islands - away, islands)
                    term = jnp.where(origin == island, terms[away], term)
                total = term if total is None else total + term
        out_ref[rows] = (p_ref[rows] - total * (1.0 / islands)).astype(out_ref.dtype)


def on_chip(kernel, out_shape, *args, name, scalars=0):
    vmem = pl.BlockSpec(memory_space=pltpu.VMEM)
    smem = pl.BlockSpec(memory_space=pltpu.SMEM)
    return pl.pallas_call(
        kernel,
        in_specs=[smem] * scalars + [vmem] * (len(args) - scalars),
        out_specs=jax.tree.map(lambda _: vmem, out_shape),
        out_shape=out_shape,
        compiler_params=pltpu.CompilerParams(vmem_limit_bytes=VMEM_LIMIT),
        cost_estimate=pl.CostEstimate(
            flops=5 * 10**8, bytes_accessed=4 * 2**20, transcendentals=0
        ),
        name=name,
    )(*args)


def local(momentum, gradient, params, indices):
    islands = lax.axis_size("island")
    _, count, length = momentum.shape
    keep = indices.shape[2]
    table = jnp.asarray(dct_table(length))
    numbers = indices[0].T
    short = numbers.astype(jnp.int16)
    rings = [
        [(i, (i + away) % islands) for i in range(islands)] for away in range(1, islands)
    ]
    other_numbers = [lax.ppermute(short, "island", ring) for ring in rings]

    tail = -(-(count // length) // 16) * 16
    packed = jax.ShapeDtypeStruct((count * keep // length + tail, length), jnp.int16)
    wide = jax.ShapeDtypeStruct((count, length), jnp.float32)
    lanes = jax.ShapeDtypeStruct((count, length), jnp.int32)
    fresh = jax.ShapeDtypeStruct((count, length), jnp.bfloat16)

    msg = on_chip(encode_kernel, packed, table, numbers, momentum[0], gradient[0], name="encode")
    other_msgs = [lax.ppermute(msg, "island", ring) for ring in rings]
    new_momentum, back = on_chip(
        own_kernel, (wide, wide), table, numbers, msg, momentum[0], gradient[0], name="own"
    )
    places = [on_chip(positions_kernel, lanes, other, name="positions") for other in other_numbers]
    me = lax.axis_index("island").astype(jnp.int32)[None]
    new_params = on_chip(
        functools.partial(finish_kernel, islands),
        fresh, me, table, back, params, *other_msgs, *places, name="finish", scalars=1,
    )
    return new_momentum[None], new_params


def solution(mesh):
    in_specs = (
        P("island", "fsdp", None),
        P("island", "fsdp", None),
        P("fsdp", None),
        P("island", "fsdp", None),
    )
    out_specs = (P("island", "fsdp", None), P("fsdp", None))
    return jax.shard_map(local, mesh=mesh, in_specs=in_specs, out_specs=out_specs, check_vma=False)
```

```python
import functools

import jax
import jax.numpy as jnp
import numpy as np
from jax import lax
from jax.experimental import pallas as pl
from jax.experimental.pallas import tpu as pltpu
from jax.sharding import PartitionSpec as P

STEPS = 32000.0
GROUPS = 4
TINY = 1e-30
WORD = 32
SUB = 8
VMEM_LIMIT = 16 * 2**20


def dct_table(length):
    freq = np.arange(length, dtype=np.float64)[:, None]
    place = np.arange(length, dtype=np.float64)[None, :]
    scale = np.where(freq == 0, np.sqrt(1.0 / length), np.sqrt(2.0 / length))
    return (scale * np.cos(np.pi * (place + 0.5) * freq / length)).astype(np.float32)


def two_parts(x):
    hi = x.astype(jnp.bfloat16)
    return hi, (x - hi.astype(jnp.float32)).astype(jnp.bfloat16)


def weights_of(table):
    hi, lo = two_parts(table)
    return jnp.concatenate(
        [jnp.concatenate([hi, lo], axis=1), jnp.concatenate([hi, jnp.zeros_like(hi)], axis=1)],
        axis=0,
    )


def transform(x, weights):
    both = jnp.dot(
        jnp.concatenate(two_parts(x), axis=1), weights, preferred_element_type=jnp.float32
    )
    length = x.shape[1]
    return both[:, :length] + both[:, length:]


def lanes_of(x, index):
    return jnp.take_along_axis(x, index, axis=1, mode="promise_in_bounds")


def row_iota():
    return lax.broadcasted_iota(jnp.int32, (SUB, 128), 0)


def mask_words(part, length):
    rows = [part[v : v + SUB] for v in range(0, part.shape[0], SUB)]
    bits = [lax.shift_left(jnp.ones_like(r), r & (WORD - 1)) for r in rows]
    words = []
    for w in range(length // WORD):
        total = None
        for r, bit in zip(rows, bits):
            term = jnp.where(lax.shift_right_logical(r, 5) == w, bit, 0)
            total = term if total is None else total + term
        for shift in (4, 2, 1):
            total = total + pltpu.roll(total, shift, 0)
        words.append(total)
    return words


def bases_of(words):
    bases = [jnp.zeros_like(words[0])]
    for word in words[:-1]:
        bases.append(bases[-1] + lax.population_count(word))
    return bases


def sorted_numbers(part, length):
    words = mask_words(part, length)
    bases = bases_of(words)
    out = []
    for v in range(0, part.shape[0], SUB):
        rank = row_iota() + v
        word, base, place = words[0], bases[0], jnp.zeros_like(rank)
        for w in range(1, len(words)):
            up = rank >= bases[w]
            word = jnp.where(up, words[w], word)
            base = jnp.where(up, bases[w], base)
            place = jnp.where(up, w * WORD, place)
        rank = rank - base
        half = WORD // 2
        while half:
            below = lax.population_count(word & ((1 << half) - 1))
            up = rank >= below
            rank = jnp.where(up, rank - below, rank)
            word = jnp.where(up, lax.shift_right_logical(word, half), word)
            place = jnp.where(up, place + half, place)
            half //= 2
        out.append(place)
    return jnp.concatenate(out, axis=0)


def positions(part, group, length):
    keep = part.shape[0]
    words = mask_words(part, length)
    bases = bases_of(words)
    out = []
    for t in range(0, length, SUB):
        place = row_iota() + t % WORD
        word = words[t // WORD]
        low = lax.shift_left(jnp.ones_like(place), place) - 1
        rank = lax.population_count(word & low) + (bases[t // WORD] + group * keep)
        held = lax.shift_right_logical(word, place) & 1
        out.append(jnp.where(held == 1, rank, -1))
    return jnp.concatenate(out, axis=0).T


def all_positions(numbers, length):
    return [
        positions(numbers[:, b * length : (b + 1) * length], b % GROUPS, length)
        for b in range(numbers.shape[1] // length)
    ]


def shorten_kernel(idx_ref, short_ref):
    short_ref[...] = idx_ref[...].astype(jnp.int16)


def order_kernel(idx_ref, picks_ref):
    length = picks_ref.shape[1]
    for c in range(picks_ref.shape[0] // length):
        picks_ref[c * length : (c + 1) * length] = jnp.concatenate(
            [
                sorted_numbers(idx_ref[:, b * length : (b + 1) * length], length)
                for b in range(c * GROUPS, (c + 1) * GROUPS)
            ],
            axis=0,
        ).T


def encode_kernel(table_ref, picks_ref, m_ref, g_ref, msg_ref):
    count, length = m_ref.shape
    keep = length // GROUPS
    weights = weights_of(table_ref[...].T)
    group = lax.broadcasted_iota(jnp.int32, (length, length), 1) // keep
    scales = []
    for c in range(count // (GROUPS * length)):
        picks = picks_ref[c * length : (c + 1) * length]
        rows = slice(c * GROUPS * length, (c + 1) * GROUPS * length)
        mom = 0.999 * m_ref[rows] + g_ref[rows].astype(jnp.float32)
        coef = transform(mom, weights)
        values = lanes_of(coef[:length], picks)
        for g in range(1, GROUPS):
            other = lanes_of(coef[g * length : (g + 1) * length], picks)
            values = jnp.where(group == g, other, values)
        turned = values.T
        coded = []
        for g in range(GROUPS):
            part = turned[g * keep : (g + 1) * keep]
            top = jnp.max(jnp.abs(part), axis=0, keepdims=True)
            power = jnp.ceil(jnp.log2(jnp.maximum(top, TINY)))
            scales.append(power)
            coded.append(jnp.round(part * (STEPS * jnp.exp2(-power))))
        msg_ref[c * length : (c + 1) * length] = (
            jnp.concatenate(coded, axis=0).astype(jnp.int32).astype(jnp.int16)
        )
    rows = msg_ref.shape[0] - count * keep // length
    if rows > len(scales):
        scales.append(jnp.zeros((rows - len(scales), length), jnp.float32))
    msg_ref[msg_ref.shape[0] - rows :] = (
        jnp.concatenate(scales, axis=0).astype(jnp.int32).astype(jnp.int16)
    )


def spread(msg_ref, lanes, c, keep):
    length = msg_ref.shape[1]
    rows = msg_ref[c * length : (c + 1) * length].astype(jnp.int32).astype(jnp.float32)
    chunks = msg_ref.shape[0] // length
    tail = msg_ref[chunks * length :].astype(jnp.int32).astype(jnp.float32)
    unit = jnp.exp2(tail[c * GROUPS : (c + 1) * GROUPS]) * (1.0 / STEPS)
    values = jnp.concatenate(
        [rows[g * keep : (g + 1) * keep] * unit[g : g + 1] for g in range(GROUPS)], axis=0
    ).T
    return jnp.concatenate(
        [jnp.where(at >= 0, lanes_of(values, at & (length - 1)), 0.0) for at in lanes], axis=0
    )


def copy_out(held_ref, out_ref, sems, c):
    size = held_ref.shape[0] // sems.shape[0]
    rows = pl.ds(c * size, size)
    return pltpu.make_async_copy(held_ref.at[rows], out_ref.at[rows], sems.at[c])


def own_kernel(table_ref, idx_ref, msg_ref, m_ref, g_ref, new_ref, back_ref, held_ref, sems):
    count, length = m_ref.shape
    keep = idx_ref.shape[0]
    weights = weights_of(table_ref[...])
    for c in range(count // (GROUPS * length)):
        rows = slice(c * GROUPS * length, (c + 1) * GROUPS * length)
        lanes = all_positions(idx_ref[:, rows], length)
        back = transform(spread(msg_ref, lanes, c, keep), weights)
        back_ref[rows] = back
        held_ref[rows] = 0.999 * m_ref[rows] + g_ref[rows].astype(jnp.float32) - back
        copy_out(held_ref, new_ref, sems, c).start()
    for c in range(sems.shape[0]):
        copy_out(held_ref, new_ref, sems, c).wait()


def positions_kernel(idx_ref, lanes_ref):
    length = lanes_ref.shape[1]
    numbers = idx_ref[...].astype(jnp.int32)
    for b, lanes in enumerate(all_positions(numbers, length)):
        lanes_ref[b * length : (b + 1) * length] = lanes


def finish_kernel(islands, me_ref, table_ref, back_ref, p_ref, *refs):
    out_ref, held_ref, sems = refs[-3:]
    msgs, places = refs[: islands - 1], refs[islands - 1 : 2 * islands - 2]
    count, length = p_ref.shape
    keep = length // GROUPS
    weights = weights_of(table_ref[...])
    for c in range(count // (GROUPS * length)):
        rows = slice(c * GROUPS * length, (c + 1) * GROUPS * length)
        terms = [back_ref[rows]]
        for msg_ref, lanes_ref in zip(msgs, places):
            lanes = [
                lanes_ref[b * length : (b + 1) * length]
                for b in range(c * GROUPS, (c + 1) * GROUPS)
            ]
            terms.append(transform(spread(msg_ref, lanes, c, keep), weights))
        if islands == 2:
            total = terms[0] + terms[1]
        else:
            total = None
            for island in range(islands):
                term = terms[0]
                for away in range(1, islands):
                    origin = lax.rem(me_ref[0] + islands - away, islands)
                    term = jnp.where(origin == island, terms[away], term)
                total = term if total is None else total + term
        held_ref[rows] = (p_ref[rows] - total * (1.0 / islands)).astype(out_ref.dtype)
        copy_out(held_ref, out_ref, sems, c).start()
    for c in range(sems.shape[0]):
        copy_out(held_ref, out_ref, sems, c).wait()


def on_chip(kernel, out_shape, *args, name, flops=5 * 10**8, scalars=0, written=None):
    vmem = pl.BlockSpec(memory_space=pltpu.VMEM)
    smem = pl.BlockSpec(memory_space=pltpu.SMEM)
    out_specs = [vmem] * len(out_shape)
    scratch = []
    if written:
        out_specs[0] = pl.BlockSpec(memory_space=pl.ANY)
        scratch = [
            pltpu.VMEM(out_shape[0].shape, out_shape[0].dtype),
            pltpu.SemaphoreType.DMA((written,)),
        ]
    return pl.pallas_call(
        kernel,
        in_specs=[smem] * scalars + [vmem] * (len(args) - scalars),
        out_specs=out_specs,
        out_shape=out_shape,
        scratch_shapes=scratch,
        compiler_params=pltpu.CompilerParams(vmem_limit_bytes=VMEM_LIMIT),
        cost_estimate=pl.CostEstimate(flops=flops, bytes_accessed=4 * 2**20, transcendentals=0),
        name=name,
    )(*args)


def local(momentum, gradient, params, indices):
    islands = lax.axis_size("island")
    _, count, length = momentum.shape
    keep = indices.shape[2]
    table = jnp.asarray(dct_table(length))
    numbers = indices[0].T
    chunks = count // (GROUPS * length)
    rings = [
        [(i, (i + away) % islands) for i in range(islands)] for away in range(1, islands)
    ]

    def array(rows, dtype):
        return jax.ShapeDtypeStruct((rows, length), dtype)

    short_shape = jax.ShapeDtypeStruct(numbers.shape, jnp.int16)
    (short,) = on_chip(shorten_kernel, [short_shape], numbers, name="shorten", flops=5 * 10**9)
    other_numbers = [lax.ppermute(short, "island", ring) for ring in rings]
    (picks,) = on_chip(order_kernel, [array(chunks * length, jnp.int32)], numbers, name="order")
    tail = -(-(count // length) // 16) * 16
    packed = array(chunks * length + tail, jnp.int16)
    (msg,) = on_chip(
        encode_kernel, [packed], table, picks, momentum[0], gradient[0], name="encode"
    )
    other_msgs = [lax.ppermute(msg, "island", ring) for ring in rings]
    wide = array(count, jnp.float32)
    new_momentum, back = on_chip(
        own_kernel, [wide, wide], table, numbers, msg, momentum[0], gradient[0],
        name="own", written=chunks,
    )
    places = [
        on_chip(positions_kernel, [array(count, jnp.int32)], other, name="positions")[0]
        for other in other_numbers
    ]
    me = lax.axis_index("island").astype(jnp.int32)[None]
    (new_params,) = on_chip(
        functools.partial(finish_kernel, islands),
        [array(count, jnp.bfloat16)], me, table, back, params, *other_msgs, *places,
        name="finish", scalars=1, written=chunks,
    )
    return new_momentum[None], new_params


def solution(mesh):
    in_specs = (
        P("island", "fsdp", None),
        P("island", "fsdp", None),
        P("fsdp", None),
        P("island", "fsdp", None),
    )
    out_specs = (P("island", "fsdp", None), P("fsdp", None))
    return jax.shard_map(local, mesh=mesh, in_specs=in_specs, out_specs=out_specs, check_vma=False)
```

```python
import functools

import jax
import jax.numpy as jnp
import numpy as np
from jax import lax
from jax.experimental import pallas as pl
from jax.experimental.pallas import tpu as pltpu
from jax.sharding import PartitionSpec as P

STEPS = 32000.0
GROUPS = 4
TINY = 1e-30
WORD = 32
SUB = 8
VMEM_LIMIT = 16 * 2**20


def dct_table(length):
    freq = np.arange(length, dtype=np.float64)[:, None]
    place = np.arange(length, dtype=np.float64)[None, :]
    scale = np.where(freq == 0, np.sqrt(1.0 / length), np.sqrt(2.0 / length))
    return (scale * np.cos(np.pi * (place + 0.5) * freq / length)).astype(np.float32)


def two_parts(x):
    hi = x.astype(jnp.bfloat16)
    return hi, (x - hi.astype(jnp.float32)).astype(jnp.bfloat16)


def weights_of(table):
    hi, lo = two_parts(table)
    return jnp.concatenate(
        [jnp.concatenate([hi, lo], axis=1), jnp.concatenate([hi, jnp.zeros_like(hi)], axis=1)],
        axis=0,
    )


def transform(x, weights):
    both = jnp.dot(
        jnp.concatenate(two_parts(x), axis=1), weights, preferred_element_type=jnp.float32
    )
    length = x.shape[1]
    return both[:, :length] + both[:, length:]


def rows_of(x, index):
    return jnp.take_along_axis(x, index, axis=0, mode="promise_in_bounds")


def row_iota():
    return lax.broadcasted_iota(jnp.int32, (SUB, 128), 0)


def mask_words(part, length):
    rows = [part[v : v + SUB] for v in range(0, part.shape[0], SUB)]
    bits = [lax.shift_left(jnp.ones_like(r), r & (WORD - 1)) for r in rows]
    words = []
    for w in range(length // WORD):
        total = None
        for r, bit in zip(rows, bits):
            term = jnp.where(lax.shift_right_logical(r, 5) == w, bit, 0)
            total = term if total is None else total + term
        for shift in (4, 2, 1):
            total = total + pltpu.roll(total, shift, 0)
        words.append(total)
    return words


def bases_of(words):
    bases = [jnp.zeros_like(words[0])]
    for word in words[:-1]:
        bases.append(bases[-1] + lax.population_count(word))
    return bases


def sorted_numbers(part, length):
    words = mask_words(part, length)
    bases = bases_of(words)
    out = []
    for v in range(0, part.shape[0], SUB):
        rank = row_iota() + v
        word, base, end = words[0], bases[0], jnp.full_like(rank, WORD)
        for w in range(1, len(words)):
            up = rank >= bases[w]
            word = jnp.where(up, words[w], word)
            base = jnp.where(up, bases[w], base)
            end = jnp.where(up, (w + 1) * WORD, end)
        rank = rank - base
        left = jnp.full_like(rank, WORD)
        half = WORD // 2
        while half:
            less = left - half
            below = lax.population_count(lax.shift_left(word, less))
            left = jnp.where(rank >= below, less, left)
            half //= 2
        out.append(end - left)
    return jnp.concatenate(out, axis=0)


def positions(part, length):
    words = mask_words(part, length)
    bases = bases_of(words)
    out = []
    for t in range(0, length, SUB):
        place = row_iota() + t % WORD
        word = words[t // WORD]
        low = lax.shift_left(jnp.ones_like(place), place) - 1
        rank = lax.population_count(word & low) + bases[t // WORD]
        held = lax.shift_right_logical(word, place) & 1
        out.append(jnp.where(held == 1, rank, -1))
    return jnp.concatenate(out, axis=0)


def choose(pieces, index):
    inner = index & (SUB - 1)
    found = {p: rows_of(x, inner) for p, x in pieces.items()}
    bit = SUB
    while len(found) > 1:
        up = (index & bit) != 0
        halves = {}
        for p in sorted({p // 2 for p in found}):
            low, high = found.get(2 * p), found.get(2 * p + 1)
            if low is None or high is None:
                halves[p] = high if low is None else low
            else:
                halves[p] = jnp.where(up, high, low)
        found = halves
        bit *= 2
    return next(iter(found.values()))


def shorten_kernel(idx_ref, short_ref):
    short_ref[...] = idx_ref[...].astype(jnp.int16)


def order_kernel(idx_ref, picks_ref):
    length = picks_ref.shape[1]
    for c in range(picks_ref.shape[0] // length):
        picks_ref[c * length : (c + 1) * length] = jnp.concatenate(
            [
                sorted_numbers(idx_ref[:, b * length : (b + 1) * length], length)
                for b in range(c * GROUPS, (c + 1) * GROUPS)
            ],
            axis=0,
        )


def encode_kernel(table_ref, picks_ref, m_ref, g_ref, msg_ref):
    count, length = m_ref.shape
    keep = length // GROUPS
    spare = (length - keep) // SUB
    weights = weights_of(table_ref[...].T)
    scales = []
    for c in range(count // (GROUPS * length)):
        rows = slice(c * GROUPS * length, (c + 1) * GROUPS * length)
        mom = 0.999 * m_ref[rows] + g_ref[rows].astype(jnp.float32)
        coef = transform(mom, weights)
        coded = []
        for g in range(GROUPS):
            turned = coef[g * length : (g + 1) * length].T
            values = []
            for v in range(keep // SUB):
                at = c * length + g * keep + v * SUB
                pieces = {p: turned[p * SUB : (p + 1) * SUB] for p in range(v, v + spare + 1)}
                values.append(choose(pieces, picks_ref[at : at + SUB]))
            part = jnp.concatenate(values, axis=0)
            top = jnp.max(jnp.abs(part), axis=0, keepdims=True)
            power = jnp.ceil(jnp.log2(jnp.maximum(top, TINY)))
            scales.append(power)
            coded.append(jnp.round(part * (STEPS * jnp.exp2(-power))))
        msg_ref[c * length : (c + 1) * length] = (
            jnp.concatenate(coded, axis=0).astype(jnp.int32).astype(jnp.int16)
        )
    rows = msg_ref.shape[0] - count * keep // length
    if rows > len(scales):
        scales.append(jnp.zeros((rows - len(scales), length), jnp.float32))
    msg_ref[msg_ref.shape[0] - rows :] = (
        jnp.concatenate(scales, axis=0).astype(jnp.int32).astype(jnp.int16)
    )


def spread(msg_ref, ranks, c, base):
    length = msg_ref.shape[1]
    keep = length // GROUPS
    spare = (length - keep) // SUB
    rows = msg_ref[c * length : (c + 1) * length].astype(jnp.int32).astype(jnp.float32)
    tail = msg_ref[base:].astype(jnp.int32).astype(jnp.float32)
    unit = jnp.exp2(tail[c * GROUPS : (c + 1) * GROUPS]) * (1.0 / STEPS)
    out = []
    for g, rank in enumerate(ranks):
        values = rows[g * keep : (g + 1) * keep] * unit[g : g + 1]
        dense = []
        for t in range(length // SUB):
            at = rank[t * SUB : (t + 1) * SUB]
            pieces = {
                p: values[p * SUB : (p + 1) * SUB]
                for p in range(max(0, t - spare), min(keep // SUB - 1, t) + 1)
            }
            dense.append(jnp.where(at >= 0, choose(pieces, at), 0.0))
        out.append(jnp.concatenate(dense, axis=0).T)
    return jnp.concatenate(out, axis=0)


def copy_out(held_ref, out_ref, sems, c):
    size = held_ref.shape[0] // sems.shape[0]
    rows = pl.ds(c * size, size)
    return pltpu.make_async_copy(held_ref.at[rows], out_ref.at[rows], sems.at[c])


def own_kernel(table_ref, idx_ref, msg_ref, m_ref, g_ref, new_ref, back_ref, held_ref, sems):
    count, length = m_ref.shape
    size = GROUPS * length
    base = count // GROUPS
    weights = weights_of(table_ref[...])
    for c in range(count // size):
        ranks = [
            positions(idx_ref[:, b * length : (b + 1) * length], length)
            for b in range(c * GROUPS, (c + 1) * GROUPS)
        ]
        rows = slice(c * size, (c + 1) * size)
        back = transform(spread(msg_ref, ranks, c, base), weights)
        back_ref[rows] = back
        held_ref[rows] = 0.999 * m_ref[rows] + g_ref[rows].astype(jnp.float32) - back
        copy_out(held_ref, new_ref, sems, c).start()
    for c in range(sems.shape[0]):
        copy_out(held_ref, new_ref, sems, c).wait()


def positions_kernel(idx_ref, ranks_ref):
    length, count = ranks_ref.shape
    numbers = idx_ref[...].astype(jnp.int32)
    for b in range(count // length):
        lanes = slice(b * length, (b + 1) * length)
        ranks_ref[:, lanes] = positions(numbers[:, lanes], length)


def finish_kernel(islands, me_ref, table_ref, back_ref, p_ref, *refs):
    out_ref, held_ref, sems = refs[-3:]
    msgs, places = refs[: islands - 1], refs[islands - 1 : 2 * islands - 2]
    count, length = p_ref.shape
    size = GROUPS * length
    base = count // GROUPS
    weights = weights_of(table_ref[...])
    for c in range(count // size):
        rows = slice(c * size, (c + 1) * size)
        terms = [back_ref[rows]]
        for msg_ref, ranks_ref in zip(msgs, places):
            ranks = [
                ranks_ref[:, b * length : (b + 1) * length]
                for b in range(c * GROUPS, (c + 1) * GROUPS)
            ]
            terms.append(transform(spread(msg_ref, ranks, c, base), weights))
        if islands == 2:
            total = terms[0] + terms[1]
        else:
            total = None
            for island in range(islands):
                term = terms[0]
                for away in range(1, islands):
                    origin = lax.rem(me_ref[0] + islands - away, islands)
                    term = jnp.where(origin == island, terms[away], term)
                total = term if total is None else total + term
        held_ref[rows] = (p_ref[rows] - total * (1.0 / islands)).astype(out_ref.dtype)
        copy_out(held_ref, out_ref, sems, c).start()
    for c in range(sems.shape[0]):
        copy_out(held_ref, out_ref, sems, c).wait()


def on_chip(kernel, out_shape, *args, name, flops=5 * 10**8, scalars=0, written=None):
    vmem = pl.BlockSpec(memory_space=pltpu.VMEM)
    smem = pl.BlockSpec(memory_space=pltpu.SMEM)
    out_specs = [vmem] * len(out_shape)
    scratch = []
    if written:
        out_specs[0] = pl.BlockSpec(memory_space=pl.ANY)
        scratch = [
            pltpu.VMEM(out_shape[0].shape, out_shape[0].dtype),
            pltpu.SemaphoreType.DMA((written,)),
        ]
    return pl.pallas_call(
        kernel,
        in_specs=[smem] * scalars + [vmem] * (len(args) - scalars),
        out_specs=out_specs,
        out_shape=out_shape,
        scratch_shapes=scratch,
        compiler_params=pltpu.CompilerParams(vmem_limit_bytes=VMEM_LIMIT),
        cost_estimate=pl.CostEstimate(flops=flops, bytes_accessed=4 * 2**20, transcendentals=0),
        name=name,
    )(*args)


def local(momentum, gradient, params, indices):
    islands = lax.axis_size("island")
    _, count, length = momentum.shape
    keep = indices.shape[2]
    table = jnp.asarray(dct_table(length))
    numbers = indices[0].T
    chunks = count // (GROUPS * length)
    rings = [
        [(i, (i + away) % islands) for i in range(islands)] for away in range(1, islands)
    ]

    def array(rows, dtype):
        return jax.ShapeDtypeStruct((rows, length), dtype)

    short_shape = jax.ShapeDtypeStruct(numbers.shape, jnp.int16)
    (short,) = on_chip(shorten_kernel, [short_shape], numbers, name="shorten", flops=5 * 10**9)
    other_numbers = [lax.ppermute(short, "island", ring) for ring in rings]
    (picks,) = on_chip(order_kernel, [array(chunks * length, jnp.int32)], numbers, name="order")
    tail = -(-(count // length) // 16) * 16
    packed = array(chunks * length + tail, jnp.int16)
    (msg,) = on_chip(
        encode_kernel, [packed], table, picks, momentum[0], gradient[0], name="encode"
    )
    other_msgs = [lax.ppermute(msg, "island", ring) for ring in rings]
    wide = array(count, jnp.float32)
    new_momentum, back = on_chip(
        own_kernel, [wide, wide], table, numbers, msg, momentum[0], gradient[0],
        name="own", written=chunks,
    )
    places = [
        on_chip(
            positions_kernel, [jax.ShapeDtypeStruct((length, count), jnp.int32)], other,
            name="positions",
        )[0]
        for other in other_numbers
    ]
    me = lax.axis_index("island").astype(jnp.int32)[None]
    (new_params,) = on_chip(
        functools.partial(finish_kernel, islands),
        [array(count, jnp.bfloat16)], me, table, back, params, *other_msgs, *places,
        name="finish", scalars=1, written=chunks,
    )
    return new_momentum[None], new_params


def solution(mesh):
    in_specs = (
        P("island", "fsdp", None),
        P("island", "fsdp", None),
        P("fsdp", None),
        P("island", "fsdp", None),
    )
    out_specs = (P("island", "fsdp", None), P("fsdp", None))
    return jax.shard_map(local, mesh=mesh, in_specs=in_specs, out_specs=out_specs, check_vma=False)
```

```python
import functools

import jax
import jax.numpy as jnp
import numpy as np
from jax import lax
from jax.experimental import pallas as pl
from jax.experimental.pallas import tpu as pltpu
from jax.sharding import PartitionSpec as P

STEPS = 32000.0
GROUPS = 4
TINY = 1e-30
WORD = 32
SUB = 8
VMEM_LIMIT = 16 * 2**20


def dct_table(length):
    freq = np.arange(length, dtype=np.float64)[:, None]
    place = np.arange(length, dtype=np.float64)[None, :]
    scale = np.where(freq == 0, np.sqrt(1.0 / length), np.sqrt(2.0 / length))
    return (scale * np.cos(np.pi * (place + 0.5) * freq / length)).astype(np.float32)


def two_parts(x):
    hi = x.astype(jnp.bfloat16)
    return hi, (x - hi.astype(jnp.float32)).astype(jnp.bfloat16)


def weights_of(table):
    hi, lo = two_parts(table)
    return jnp.concatenate(
        [jnp.concatenate([hi, lo], axis=1), jnp.concatenate([hi, jnp.zeros_like(hi)], axis=1)],
        axis=0,
    )


def transform(x, weights):
    both = jnp.dot(
        jnp.concatenate(two_parts(x), axis=1), weights, preferred_element_type=jnp.float32
    )
    length = x.shape[1]
    return both[:, :length] + both[:, length:]


def rows_of(x, index):
    return jnp.take_along_axis(x, index, axis=0, mode="promise_in_bounds")


def row_iota():
    return lax.broadcasted_iota(jnp.int32, (SUB, 128), 0)


def mask_words(part, length):
    rows = [part[v : v + SUB] for v in range(0, part.shape[0], SUB)]
    bits = [lax.shift_left(jnp.ones_like(r), r & (WORD - 1)) for r in rows]
    words = []
    for w in range(length // WORD):
        total = None
        for r, bit in zip(rows, bits):
            term = jnp.where(lax.shift_right_logical(r, 5) == w, bit, 0)
            total = term if total is None else total + term
        for shift in (4, 2, 1):
            total = total + pltpu.roll(total, shift, 0)
        words.append(total)
    return words


def bases_of(words):
    bases = [jnp.zeros_like(words[0])]
    for word in words[:-1]:
        bases.append(bases[-1] + lax.population_count(word))
    return bases


def sorted_numbers(part, length):
    words = mask_words(part, length)
    bases = bases_of(words)
    out = []
    for v in range(0, part.shape[0], SUB):
        rank = row_iota() + v
        word, base, end = words[0], bases[0], jnp.full_like(rank, WORD)
        for w in range(1, len(words)):
            up = rank >= bases[w]
            word = jnp.where(up, words[w], word)
            base = jnp.where(up, bases[w], base)
            end = jnp.where(up, (w + 1) * WORD, end)
        rank = rank - base
        left = jnp.full_like(rank, WORD)
        half = WORD // 2
        while half:
            less = left - half
            below = lax.population_count(lax.shift_left(word, less))
            left = jnp.where(rank >= below, less, left)
            half //= 2
        out.append(end - left)
    return jnp.concatenate(out, axis=0)


def positions(part, length):
    words = mask_words(part, length)
    bases = bases_of(words)
    out = []
    for t in range(0, length, SUB):
        place = row_iota() + t % WORD
        word = words[t // WORD]
        low = lax.shift_left(jnp.ones_like(place), place) - 1
        rank = lax.population_count(word & low) + bases[t // WORD]
        held = lax.shift_right_logical(word, place) & 1
        out.append(jnp.where(held == 1, rank, -1))
    return jnp.concatenate(out, axis=0)


def choose(pieces, index):
    inner = index & (SUB - 1)
    found = {p: rows_of(x, inner) for p, x in pieces.items()}
    bit = SUB
    while len(found) > 1:
        up = (index & bit) != 0
        halves = {}
        for p in sorted({p // 2 for p in found}):
            low, high = found.get(2 * p), found.get(2 * p + 1)
            if low is None or high is None:
                halves[p] = high if low is None else low
            else:
                halves[p] = jnp.where(up, high, low)
        found = halves
        bit *= 2
    return next(iter(found.values()))


def shorten_kernel(idx_ref, short_ref):
    short_ref[...] = idx_ref[...].astype(jnp.int16)


def order_kernel(short_ref, picks_ref):
    length = picks_ref.shape[1]
    numbers = short_ref[...].astype(jnp.int32)
    for c in range(picks_ref.shape[0] // length):
        picks_ref[c * length : (c + 1) * length] = jnp.concatenate(
            [
                sorted_numbers(numbers[:, b * length : (b + 1) * length], length)
                for b in range(c * GROUPS, (c + 1) * GROUPS)
            ],
            axis=0,
        )


def encode_kernel(chunks, table_ref, picks_ref, m_ref, g_ref, msg_ref):
    length = m_ref.shape[1]
    keep = length // GROUPS
    spare = (length - keep) // SUB
    weights = weights_of(table_ref[...].T)
    scales = []
    for i, c in enumerate(chunks):
        rows = slice(c * GROUPS * length, (c + 1) * GROUPS * length)
        mom = 0.999 * m_ref[rows] + g_ref[rows].astype(jnp.float32)
        coef = transform(mom, weights)
        coded = []
        for g in range(GROUPS):
            turned = coef[g * length : (g + 1) * length].T
            values = []
            for v in range(keep // SUB):
                at = c * length + g * keep + v * SUB
                pieces = {p: turned[p * SUB : (p + 1) * SUB] for p in range(v, v + spare + 1)}
                values.append(choose(pieces, picks_ref[at : at + SUB]))
            part = jnp.concatenate(values, axis=0)
            top = jnp.max(jnp.abs(part), axis=0, keepdims=True)
            power = jnp.ceil(jnp.log2(jnp.maximum(top, TINY)))
            scales.append(power)
            coded.append(jnp.round(part * (STEPS * jnp.exp2(-power))))
        msg_ref[i * length : (i + 1) * length] = (
            jnp.concatenate(coded, axis=0).astype(jnp.int32).astype(jnp.int16)
        )
    base = len(chunks) * length
    rows = msg_ref.shape[0] - base
    if rows > len(scales):
        scales.append(jnp.zeros((rows - len(scales), length), jnp.float32))
    msg_ref[base:] = jnp.concatenate(scales, axis=0).astype(jnp.int32).astype(jnp.int16)


def spread(msg_ref, ranks, i, base):
    length = msg_ref.shape[1]
    keep = length // GROUPS
    spare = (length - keep) // SUB
    rows = msg_ref[i * length : (i + 1) * length].astype(jnp.int32).astype(jnp.float32)
    tail = msg_ref[base:].astype(jnp.int32).astype(jnp.float32)
    unit = jnp.exp2(tail[i * GROUPS : (i + 1) * GROUPS]) * (1.0 / STEPS)
    out = []
    for g, rank in enumerate(ranks):
        values = rows[g * keep : (g + 1) * keep] * unit[g : g + 1]
        dense = []
        for t in range(length // SUB):
            at = rank[t * SUB : (t + 1) * SUB]
            pieces = {
                p: values[p * SUB : (p + 1) * SUB]
                for p in range(max(0, t - spare), min(keep // SUB - 1, t) + 1)
            }
            dense.append(jnp.where(at >= 0, choose(pieces, at), 0.0))
        out.append(jnp.concatenate(dense, axis=0).T)
    return jnp.concatenate(out, axis=0)


def copy_out(held_ref, out_ref, sem, base, rows):
    place = pl.ds(base + rows.start, rows.stop - rows.start)
    return pltpu.make_async_copy(
        held_ref.at[pl.ds(rows.start, rows.stop - rows.start)], out_ref.at[place], sem
    )


def own_kernel(parts, islands, table_ref, short_ref, m_ref, g_ref, *refs):
    msgs, refs = refs[: len(parts)], refs[len(parts) :]
    others, refs = refs[: islands - 1], refs[islands - 1 :]
    new_ref, back_ref = refs[:2]
    places = refs[2:]
    length = m_ref.shape[1]
    size = GROUPS * length
    weights = weights_of(table_ref[...])
    numbers = short_ref[...].astype(jnp.int32)
    for chunks, msg_ref in zip(parts, msgs):
        for i, c in enumerate(chunks):
            ranks = [
                positions(numbers[:, b * length : (b + 1) * length], length)
                for b in range(c * GROUPS, (c + 1) * GROUPS)
            ]
            rows = slice(c * size, (c + 1) * size)
            back = transform(spread(msg_ref, ranks, i, len(chunks) * length), weights)
            back_ref[rows] = back
            new_ref[rows] = 0.999 * m_ref[rows] + g_ref[rows].astype(jnp.float32) - back
    for other_ref, ranks_ref in zip(others, places):
        numbers = other_ref[...].astype(jnp.int32)
        for b in range(numbers.shape[1] // length):
            lanes = slice(b * length, (b + 1) * length)
            ranks_ref[:, lanes] = positions(numbers[:, lanes], length)


def finish_kernel(parts, islands, me_ref, table_ref, back_ref, p_ref, *refs):
    msgs, refs = refs[: islands - 1], refs[islands - 1 :]
    places, refs = refs[: islands - 1], refs[islands - 1 :]
    chunks = parts[-1]
    length = p_ref.shape[1]
    size = GROUPS * length
    last = chunks.stop * size == p_ref.shape[0]
    first = chunks.start * size
    copies = []
    if last:
        new_ref, *earlier, out_ref, new_out_ref, held_ref, sems = refs
        copies.append(pltpu.make_async_copy(new_ref, new_out_ref, sems.at[sems.shape[0] - 1]))
        copies[-1].start()
        for i, (part, early_ref) in enumerate(zip(parts, earlier)):
            rows = slice(0, early_ref.shape[0])
            copies.append(copy_out(early_ref, out_ref, sems.at[i], part.start * size, rows))
            copies[-1].start()
    else:
        (held_ref,) = refs
    weights = weights_of(table_ref[...])
    for i, c in enumerate(chunks):
        rows = slice(c * size, (c + 1) * size)
        terms = [back_ref[rows]]
        for msg_ref, ranks_ref in zip(msgs, places):
            ranks = [
                ranks_ref[:, b * length : (b + 1) * length]
                for b in range(c * GROUPS, (c + 1) * GROUPS)
            ]
            kept = spread(msg_ref, ranks, i, len(chunks) * length)
            terms.append(transform(kept, weights))
        if islands == 2:
            total = terms[0] + terms[1]
        else:
            total = None
            for island in range(islands):
                term = terms[0]
                for away in range(1, islands):
                    origin = lax.rem(me_ref[0] + islands - away, islands)
                    term = jnp.where(origin == island, terms[away], term)
                total = term if total is None else total + term
        done = slice(i * size, (i + 1) * size)
        held_ref[done] = (p_ref[rows] - total * (1.0 / islands)).astype(held_ref.dtype)
        if last:
            sem = sems.at[len(parts) - 1 + i]
            copies.append(copy_out(held_ref, out_ref, sem, first, done))
            copies[-1].start()
    for copy in copies:
        copy.wait()


def on_chip(kernel, out_shape, *args, name, flops=5 * 10**8, scalars=0, held=None, copies=0):
    vmem = pl.BlockSpec(memory_space=pltpu.VMEM)
    smem = pl.BlockSpec(memory_space=pltpu.SMEM)
    out_specs = [vmem] * len(out_shape)
    scratch = []
    if copies:
        out_specs = [pl.BlockSpec(memory_space=pl.ANY)] * len(out_shape)
        scratch = [pltpu.VMEM(held.shape, held.dtype), pltpu.SemaphoreType.DMA((copies,))]
    return pl.pallas_call(
        kernel,
        in_specs=[smem] * scalars + [vmem] * (len(args) - scalars),
        out_specs=out_specs,
        out_shape=out_shape,
        scratch_shapes=scratch,
        compiler_params=pltpu.CompilerParams(vmem_limit_bytes=VMEM_LIMIT),
        cost_estimate=pl.CostEstimate(flops=flops, bytes_accessed=4 * 2**20, transcendentals=0),
        name=name,
    )(*args)


def local(momentum, gradient, params, indices):
    islands = lax.axis_size("island")
    _, count, length = momentum.shape
    table = jnp.asarray(dct_table(length))
    numbers = indices[0].T
    chunks = count // (GROUPS * length)
    parts = [part for part in (range(chunks - 1), range(chunks - 1, chunks)) if len(part)]
    rings = [
        [(i, (i + away) % islands) for i in range(islands)] for away in range(1, islands)
    ]

    def array(rows, dtype, lanes=length):
        return jax.ShapeDtypeStruct((rows, lanes), dtype)

    def to_others(x):
        return [lax.ppermute(x, "island", ring) for ring in rings]

    (short,) = on_chip(
        shorten_kernel, [array(numbers.shape[0], jnp.int16, count)], numbers,
        name="shorten", flops=5 * 10**9,
    )
    other_numbers = to_others(short)
    (picks,) = on_chip(order_kernel, [array(chunks * length, jnp.int32)], short, name="order")
    msgs = []
    other_msgs = []
    for part in parts:
        tail = -(-(len(part) * GROUPS) // 16) * 16
        (msg,) = on_chip(
            functools.partial(encode_kernel, part),
            [array(len(part) * length + tail, jnp.int16)],
            table, picks, momentum[0], gradient[0],
            name="encode",
        )
        msgs.append(msg)
        other_msgs.append(to_others(msg))
    wide = array(count, jnp.float32)
    new, back, *places = on_chip(
        functools.partial(own_kernel, parts, islands),
        [wide, wide] + [array(length, jnp.int32, count)] * (islands - 1),
        table, short, momentum[0], gradient[0], *msgs, *other_numbers,
        name="own",
    )
    me = lax.axis_index("island").astype(jnp.int32)[None]
    fresh = []
    for i, (part, others) in enumerate(zip(parts, other_msgs)):
        last = i == len(parts) - 1
        mine = array(len(part) * GROUPS * length, jnp.bfloat16)
        results = on_chip(
            functools.partial(finish_kernel, parts[: i + 1], islands),
            [array(count, jnp.bfloat16), wide] if last else [mine],
            me, table, back, params, *others, *places, *([new] + fresh if last else []),
            name="finish", scalars=1, held=mine, copies=(i + len(part) + 1) * last,
        )
        fresh.append(results[0])
    new_params, new_momentum = results
    return new_momentum[None], new_params


def solution(mesh):
    in_specs = (
        P("island", "fsdp", None),
        P("island", "fsdp", None),
        P("fsdp", None),
        P("island", "fsdp", None),
    )
    out_specs = (P("island", "fsdp", None), P("fsdp", None))
    return jax.shard_map(local, mesh=mesh, in_specs=in_specs, out_specs=out_specs, check_vma=False)
```

```python
import functools
import math

import jax
import jax.numpy as jnp
from jax import lax
from jax.experimental import pallas as pl
from jax.experimental.pallas import tpu as pltpu
from jax.sharding import PartitionSpec as P

STEPS = 32000.0
GROUPS = 4
TINY = 1e-30
WORD = 32
SUB = 8
VMEM_LIMIT = 16 * 2**20


def dct_table(length):
    freq = lax.broadcasted_iota(jnp.int32, (length, length), 0)
    place = lax.broadcasted_iota(jnp.int32, (length, length), 1)
    turn = ((2 * place + 1) * freq) & (4 * length - 1)
    x = (jnp.abs(turn - 2 * length) - length).astype(jnp.float32) * (math.pi / (2 * length))
    square = x * x
    series = jnp.full_like(x, 1.0 / math.factorial(15))
    for n in range(13, 0, -2):
        series = 1.0 / math.factorial(n) - square * series
    scale = jnp.where(freq == 0, math.sqrt(1.0 / length), math.sqrt(2.0 / length))
    return scale * (x * series)


def two_parts(x):
    hi = x.astype(jnp.bfloat16)
    return hi, (x - hi.astype(jnp.float32)).astype(jnp.bfloat16)


def weights_of(table):
    hi, lo = two_parts(table)
    return jnp.concatenate(
        [jnp.concatenate([hi, lo], axis=1), jnp.concatenate([hi, jnp.zeros_like(hi)], axis=1)],
        axis=0,
    )


def transform(x, weights):
    both = jnp.dot(
        jnp.concatenate(two_parts(x), axis=1), weights, preferred_element_type=jnp.float32
    )
    length = x.shape[1]
    return both[:, :length] + both[:, length:]


def rows_of(x, index):
    return jnp.take_along_axis(x, index, axis=0, mode="promise_in_bounds")


def row_iota():
    return lax.broadcasted_iota(jnp.int32, (SUB, 128), 0)


def mask_words(part, length):
    rows = [part[v : v + SUB] for v in range(0, part.shape[0], SUB)]
    bits = [lax.shift_left(jnp.ones_like(r), r & (WORD - 1)) for r in rows]
    words = []
    for w in range(length // WORD):
        total = None
        for r, bit in zip(rows, bits):
            term = jnp.where(lax.shift_right_logical(r, 5) == w, bit, 0)
            total = term if total is None else total + term
        for shift in (4, 2, 1):
            total = total + pltpu.roll(total, shift, 0)
        words.append(total)
    return words


def bases_of(words):
    bases = [jnp.zeros_like(words[0])]
    for word in words[:-1]:
        bases.append(bases[-1] + lax.population_count(word))
    return bases


def sorted_numbers(part, length):
    words = mask_words(part, length)
    bases = bases_of(words)
    out = []
    for v in range(0, part.shape[0], SUB):
        rank = row_iota() + v
        word, base, end = words[0], bases[0], jnp.full_like(rank, WORD)
        for w in range(1, len(words)):
            up = rank >= bases[w]
            word = jnp.where(up, words[w], word)
            base = jnp.where(up, bases[w], base)
            end = jnp.where(up, (w + 1) * WORD, end)
        rank = rank - base
        left = jnp.full_like(rank, WORD)
        half = WORD // 2
        while half:
            less = left - half
            below = lax.population_count(lax.shift_left(word, less))
            left = jnp.where(rank >= below, less, left)
            half //= 2
        out.append(end - left)
    return jnp.concatenate(out, axis=0)


def positions(part, length):
    words = mask_words(part, length)
    bases = bases_of(words)
    out = []
    for t in range(0, length, SUB):
        place = row_iota() + t % WORD
        word = words[t // WORD]
        low = lax.shift_left(jnp.ones_like(place), place) - 1
        rank = lax.population_count(word & low) + bases[t // WORD]
        held = lax.shift_right_logical(word, place) & 1
        out.append(jnp.where(held == 1, rank, -1))
    return jnp.concatenate(out, axis=0)


def choose(pieces, index):
    inner = index & (SUB - 1)
    found = {p: rows_of(x, inner) for p, x in pieces.items()}
    bit = SUB
    while len(found) > 1:
        up = (index & bit) != 0
        halves = {}
        for p in sorted({p // 2 for p in found}):
            low, high = found.get(2 * p), found.get(2 * p + 1)
            if low is None or high is None:
                halves[p] = high if low is None else low
            else:
                halves[p] = jnp.where(up, high, low)
        found = halves
        bit *= 2
    return next(iter(found.values()))


def prepare(numbers, picks_ref, forward_ref, inverse_ref):
    length = picks_ref.shape[1]
    table = dct_table(length)
    forward_ref[...] = weights_of(table.T)
    inverse_ref[...] = weights_of(table)
    for c in range(picks_ref.shape[0] // length):
        picks_ref[c * length : (c + 1) * length] = jnp.concatenate(
            [
                sorted_numbers(numbers[:, b * length : (b + 1) * length], length)
                for b in range(c * GROUPS, (c + 1) * GROUPS)
            ],
            axis=0,
        )


def shorten_kernel(idx_ref, short_ref, *prepared):
    short_ref[...] = idx_ref[...].astype(jnp.int16)

    @pl.when(lax.axis_index("island") == 0)
    def _():
        prepare(idx_ref[...], *prepared)


def order_kernel(short_ref, *refs):
    @pl.when(lax.axis_index("island") != 0)
    def _():
        prepare(short_ref[...].astype(jnp.int32), *refs[len(refs) // 2 :])


def encode_kernel(chunks, weights_ref, picks_ref, m_ref, g_ref, msg_ref):
    length = m_ref.shape[1]
    keep = length // GROUPS
    spare = (length - keep) // SUB
    weights = weights_ref[...]
    scales = []
    for i, c in enumerate(chunks):
        rows = slice(c * GROUPS * length, (c + 1) * GROUPS * length)
        mom = 0.999 * m_ref[rows] + g_ref[rows].astype(jnp.float32)
        coef = transform(mom, weights)
        coded = []
        for g in range(GROUPS):
            turned = coef[g * length : (g + 1) * length].T
            values = []
            for v in range(keep // SUB):
                at = c * length + g * keep + v * SUB
                pieces = {p: turned[p * SUB : (p + 1) * SUB] for p in range(v, v + spare + 1)}
                values.append(choose(pieces, picks_ref[at : at + SUB]))
            part = jnp.concatenate(values, axis=0)
            top = jnp.max(jnp.abs(part), axis=0, keepdims=True)
            power = jnp.ceil(jnp.log2(jnp.maximum(top, TINY)))
            scales.append(power)
            coded.append(jnp.round(part * (STEPS * jnp.exp2(-power))))
        msg_ref[i * length : (i + 1) * length] = (
            jnp.concatenate(coded, axis=0).astype(jnp.int32).astype(jnp.int16)
        )
    base = len(chunks) * length
    rows = msg_ref.shape[0] - base
    if rows > len(scales):
        scales.append(jnp.zeros((rows - len(scales), length), jnp.float32))
    msg_ref[base:] = jnp.concatenate(scales, axis=0).astype(jnp.int32).astype(jnp.int16)


def spread(msg_ref, ranks, i, base):
    length = msg_ref.shape[1]
    keep = length // GROUPS
    spare = (length - keep) // SUB
    rows = msg_ref[i * length : (i + 1) * length].astype(jnp.int32).astype(jnp.float32)
    tail = msg_ref[base:].astype(jnp.int32).astype(jnp.float32)
    unit = jnp.exp2(tail[i * GROUPS : (i + 1) * GROUPS]) * (1.0 / STEPS)
    out = []
    for g, rank in enumerate(ranks):
        values = rows[g * keep : (g + 1) * keep] * unit[g : g + 1]
        dense = []
        for t in range(length // SUB):
            at = rank[t * SUB : (t + 1) * SUB]
            pieces = {
                p: values[p * SUB : (p + 1) * SUB]
                for p in range(max(0, t - spare), min(keep // SUB - 1, t) + 1)
            }
            dense.append(jnp.where(at >= 0, choose(pieces, at), 0.0))
        out.append(jnp.concatenate(dense, axis=0).T)
    return jnp.concatenate(out, axis=0)


def copy_out(held_ref, out_ref, sem, base, rows):
    place = pl.ds(base + rows.start, rows.stop - rows.start)
    return pltpu.make_async_copy(
        held_ref.at[pl.ds(rows.start, rows.stop - rows.start)], out_ref.at[place], sem
    )


def own_kernel(parts, weights_ref, short_ref, m_ref, g_ref, *refs):
    msgs, refs = refs[: len(parts)], refs[len(parts) :]
    new_ref, back_ref = refs
    length = m_ref.shape[1]
    size = GROUPS * length
    weights = weights_ref[...]
    numbers = short_ref[...].astype(jnp.int32)
    for chunks, msg_ref in zip(parts, msgs):
        for i, c in enumerate(chunks):
            ranks = [
                positions(numbers[:, b * length : (b + 1) * length], length)
                for b in range(c * GROUPS, (c + 1) * GROUPS)
            ]
            rows = slice(c * size, (c + 1) * size)
            back = transform(spread(msg_ref, ranks, i, len(chunks) * length), weights)
            back_ref[rows] = back
            new_ref[rows] = 0.999 * m_ref[rows] + g_ref[rows].astype(jnp.float32) - back


def positions_kernel(others, new_ref, *refs):
    shorts, (new_out_ref, *places, sem) = refs[:others], refs[others:]
    copy = pltpu.make_async_copy(new_ref, new_out_ref, sem.at[0])
    copy.start()
    for short_ref, ranks_ref in zip(shorts, places):
        length, count = ranks_ref.shape
        numbers = short_ref[...].astype(jnp.int32)
        for b in range(count // length):
            lanes = slice(b * length, (b + 1) * length)
            ranks_ref[:, lanes] = positions(numbers[:, lanes], length)
    copy.wait()


def finish_kernel(parts, islands, me_ref, weights_ref, back_ref, p_ref, *refs):
    msgs, refs = refs[: islands - 1], refs[islands - 1 :]
    places, refs = refs[: islands - 1], refs[islands - 1 :]
    chunks = parts[-1]
    length = p_ref.shape[1]
    size = GROUPS * length
    last = chunks.stop * size == p_ref.shape[0]
    first = chunks.start * size
    copies = []
    if last:
        *earlier, out_ref, held_ref, sems = refs
        for i, (part, early_ref) in enumerate(zip(parts, earlier)):
            rows = slice(0, early_ref.shape[0])
            copies.append(copy_out(early_ref, out_ref, sems.at[i], part.start * size, rows))
            copies[-1].start()
    else:
        (held_ref,) = refs
    weights = weights_ref[...]
    for i, c in enumerate(chunks):
        rows = slice(c * size, (c + 1) * size)
        terms = [back_ref[rows]]
        for msg_ref, ranks_ref in zip(msgs, places):
            ranks = [
                ranks_ref[:, b * length : (b + 1) * length]
                for b in range(c * GROUPS, (c + 1) * GROUPS)
            ]
            kept = spread(msg_ref, ranks, i, len(chunks) * length)
            terms.append(transform(kept, weights))
        if islands == 2:
            total = terms[0] + terms[1]
        else:
            total = None
            for island in range(islands):
                term = terms[0]
                for away in range(1, islands):
                    origin = lax.rem(me_ref[0] + islands - away, islands)
                    term = jnp.where(origin == island, terms[away], term)
                total = term if total is None else total + term
        done = slice(i * size, (i + 1) * size)
        held_ref[done] = (p_ref[rows] - total * (1.0 / islands)).astype(held_ref.dtype)
        if last:
            sem = sems.at[len(parts) - 1 + i]
            copies.append(copy_out(held_ref, out_ref, sem, first, done))
            copies[-1].start()
    for copy in copies:
        copy.wait()


def on_chip(
    kernel, out_shape, *args, name, flops=5 * 10**8, scalars=0, held=None, copies=0, onto={}
):
    vmem = pl.BlockSpec(memory_space=pltpu.VMEM)
    smem = pl.BlockSpec(memory_space=pltpu.SMEM)
    out_specs = [vmem] * len(out_shape)
    scratch = []
    if copies:
        out_specs[0] = pl.BlockSpec(memory_space=pl.ANY)
        scratch = [] if held is None else [pltpu.VMEM(held.shape, held.dtype)]
        scratch.append(pltpu.SemaphoreType.DMA((copies,)))
    return pl.pallas_call(
        kernel,
        in_specs=[smem] * scalars + [vmem] * (len(args) - scalars),
        out_specs=out_specs,
        out_shape=out_shape,
        scratch_shapes=scratch,
        input_output_aliases=onto,
        compiler_params=pltpu.CompilerParams(vmem_limit_bytes=VMEM_LIMIT),
        cost_estimate=pl.CostEstimate(flops=flops, bytes_accessed=flops // 128, transcendentals=0),
        name=name,
    )(*args)


def local(momentum, gradient, params, indices):
    islands = lax.axis_size("island")
    _, count, length = momentum.shape
    numbers = indices[0].T
    chunks = count // (GROUPS * length)
    parts = [part for part in (range(chunks - 1), range(chunks - 1, chunks)) if len(part)]
    rings = [
        [(i, (i + away) % islands) for i in range(islands)] for away in range(1, islands)
    ]

    def array(rows, dtype, lanes=length):
        return jax.ShapeDtypeStruct((rows, lanes), dtype)

    def to_others(x):
        return [lax.ppermute(x, "island", ring) for ring in rings]

    weights = array(2 * length, jnp.bfloat16, 2 * length)
    prepared = [array(chunks * length, jnp.int32), weights, weights]
    short, *early = on_chip(
        shorten_kernel, [array(numbers.shape[0], jnp.int16, count)] + prepared, numbers,
        name="shorten", flops=5 * 10**9,
    )
    other_numbers = to_others(short)
    picks, forward, inverse = on_chip(
        order_kernel, prepared, short, *early,
        name="order", flops=10**4, onto={1: 0, 2: 1, 3: 2},
    )
    msgs = []
    other_msgs = []
    for part in parts:
        tail = -(-(len(part) * GROUPS) // 16) * 16
        (msg,) = on_chip(
            functools.partial(encode_kernel, part),
            [array(len(part) * length + tail, jnp.int16)],
            forward, picks, momentum[0], gradient[0],
            name="encode",
        )
        msgs.append(msg)
        other_msgs.append(to_others(msg))
    wide = array(count, jnp.float32)
    new, back = on_chip(
        functools.partial(own_kernel, parts), [wide, wide],
        inverse, short, momentum[0], gradient[0], *msgs,
        name="own",
    )
    new_momentum, *places = on_chip(
        functools.partial(positions_kernel, islands - 1),
        [wide] + [array(length, jnp.int32, count)] * (islands - 1), new, *other_numbers,
        name="positions", copies=1,
    )
    me = lax.axis_index("island").astype(jnp.int32)[None]
    fresh = []
    for i, (part, others) in enumerate(zip(parts, other_msgs)):
        last = i == len(parts) - 1
        mine = array(len(part) * GROUPS * length, jnp.bfloat16)
        (done,) = on_chip(
            functools.partial(finish_kernel, parts[: i + 1], islands),
            [array(count, jnp.bfloat16) if last else mine],
            me, inverse, back, params, *others, *places, *(fresh if last else []),
            name="finish", scalars=1, held=mine, copies=(i + len(part)) * last,
        )
        fresh.append(done)
    return new_momentum[None], fresh[-1]


def solution(mesh):
    in_specs = (
        P("island", "fsdp", None),
        P("island", "fsdp", None),
        P("fsdp", None),
        P("island", "fsdp", None),
    )
    out_specs = (P("island", "fsdp", None), P("fsdp", None))
    return jax.shard_map(local, mesh=mesh, in_specs=in_specs, out_specs=out_specs, check_vma=False)
```

```python
import functools
import math

import jax
import jax.numpy as jnp
from jax import lax
from jax.experimental import pallas as pl
from jax.experimental.pallas import tpu as pltpu
from jax.sharding import PartitionSpec as P

STEPS = 32000.0
GROUPS = 4
TINY = 1e-30
WORD = 32
SUB = 8
VMEM_LIMIT = 16 * 2**20


def dct_table(length):
    freq = lax.broadcasted_iota(jnp.int32, (length, length), 0)
    place = lax.broadcasted_iota(jnp.int32, (length, length), 1)
    turn = ((2 * place + 1) * freq) & (4 * length - 1)
    x = (jnp.abs(turn - 2 * length) - length).astype(jnp.float32) * (math.pi / (2 * length))
    square = x * x
    series = jnp.full_like(x, 1.0 / math.factorial(15))
    for n in range(13, 0, -2):
        series = 1.0 / math.factorial(n) - square * series
    scale = jnp.where(freq == 0, math.sqrt(1.0 / length), math.sqrt(2.0 / length))
    return scale * (x * series)


def two_parts(x):
    hi = x.astype(jnp.bfloat16)
    return hi, (x - hi.astype(jnp.float32)).astype(jnp.bfloat16)


def weights_of(table):
    hi, lo = two_parts(table)
    return jnp.concatenate(
        [jnp.concatenate([hi, lo], axis=1), jnp.concatenate([hi, jnp.zeros_like(hi)], axis=1)],
        axis=0,
    )


def transform(x, weights):
    both = jnp.dot(
        jnp.concatenate(two_parts(x), axis=1), weights, preferred_element_type=jnp.float32
    )
    length = x.shape[1]
    return both[:, :length] + both[:, length:]


def rows_of(x, index):
    return jnp.take_along_axis(x, index, axis=0, mode="promise_in_bounds")


def row_iota():
    return lax.broadcasted_iota(jnp.int32, (SUB, 128), 0)


def mask_words(part, length):
    rows = [part[v : v + SUB] for v in range(0, part.shape[0], SUB)]
    bits = [lax.shift_left(jnp.ones_like(r), r & (WORD - 1)) for r in rows]
    words = []
    for w in range(length // WORD):
        total = None
        for r, bit in zip(rows, bits):
            term = jnp.where(lax.shift_right_logical(r, 5) == w, bit, 0)
            total = term if total is None else total + term
        for shift in (4, 2, 1):
            total = total + pltpu.roll(total, shift, 0)
        words.append(total)
    return words


def bases_of(words):
    bases = [jnp.zeros_like(words[0])]
    for word in words[:-1]:
        bases.append(bases[-1] + lax.population_count(word))
    return bases


def sorted_numbers(part, length):
    words = mask_words(part, length)
    bases = bases_of(words)
    out = []
    for v in range(0, part.shape[0], SUB):
        rank = row_iota() + v
        word, base, end = words[0], bases[0], jnp.full_like(rank, WORD)
        for w in range(1, len(words)):
            up = rank >= bases[w]
            word = jnp.where(up, words[w], word)
            base = jnp.where(up, bases[w], base)
            end = jnp.where(up, (w + 1) * WORD, end)
        rank = rank - base
        left = jnp.full_like(rank, WORD)
        half = WORD // 2
        while half:
            less = left - half
            below = lax.population_count(lax.shift_left(word, less))
            left = jnp.where(rank >= below, less, left)
            half //= 2
        out.append(end - left)
    return jnp.concatenate(out, axis=0)


def positions(part, length):
    words = mask_words(part, length)
    bases = bases_of(words)
    out = []
    for t in range(0, length, SUB):
        place = row_iota() + t % WORD
        word = words[t // WORD]
        low = lax.shift_left(jnp.ones_like(place), place) - 1
        rank = lax.population_count(word & low) + bases[t // WORD]
        held = lax.shift_right_logical(word, place) & 1
        out.append(jnp.where(held == 1, rank, -1))
    return jnp.concatenate(out, axis=0)


def choose(pieces, index):
    inner = index & (SUB - 1)
    found = {p: rows_of(x, inner) for p, x in pieces.items()}
    bit = SUB
    while len(found) > 1:
        up = (index & bit) != 0
        halves = {}
        for p in sorted({p // 2 for p in found}):
            low, high = found.get(2 * p), found.get(2 * p + 1)
            if low is None or high is None:
                halves[p] = high if low is None else low
            else:
                halves[p] = jnp.where(up, high, low)
        found = halves
        bit *= 2
    return next(iter(found.values()))


def prepare(numbers, picks_ref, forward_ref, inverse_ref):
    length = picks_ref.shape[1]
    table = dct_table(length)
    forward_ref[...] = weights_of(table.T)
    inverse_ref[...] = weights_of(table)
    for c in range(picks_ref.shape[0] // length):
        picks_ref[c * length : (c + 1) * length] = jnp.concatenate(
            [
                sorted_numbers(numbers[:, b * length : (b + 1) * length], length)
                for b in range(c * GROUPS, (c + 1) * GROUPS)
            ],
            axis=0,
        )


def shorten_kernel(idx_ref, short_ref, *prepared):
    short_ref[...] = idx_ref[...].astype(jnp.int16)

    @pl.when(lax.axis_index("island") == 0)
    def _():
        prepare(idx_ref[...], *prepared)


def order_kernel(short_ref, *refs):
    @pl.when(lax.axis_index("island") != 0)
    def _():
        prepare(short_ref[...].astype(jnp.int32), *refs[len(refs) // 2 :])


def encode_kernel(chunks, weights_ref, picks_ref, m_ref, g_ref, msg_ref):
    length = m_ref.shape[1]
    keep = length // GROUPS
    spare = (length - keep) // SUB
    weights = weights_ref[...]
    scales = []
    for i, c in enumerate(chunks):
        rows = slice(c * GROUPS * length, (c + 1) * GROUPS * length)
        mom = 0.999 * m_ref[rows] + g_ref[rows].astype(jnp.float32)
        coef = transform(mom, weights)
        coded = []
        for g in range(GROUPS):
            turned = coef[g * length : (g + 1) * length].T
            values = []
            for v in range(keep // SUB):
                at = c * length + g * keep + v * SUB
                pieces = {p: turned[p * SUB : (p + 1) * SUB] for p in range(v, v + spare + 1)}
                values.append(choose(pieces, picks_ref[at : at + SUB]))
            part = jnp.concatenate(values, axis=0)
            top = jnp.max(jnp.abs(part), axis=0, keepdims=True)
            power = jnp.ceil(jnp.log2(jnp.maximum(top, TINY)))
            scales.append(power)
            coded.append(jnp.round(part * (STEPS * jnp.exp2(-power))))
        msg_ref[i * length : (i + 1) * length] = (
            jnp.concatenate(coded, axis=0).astype(jnp.int32).astype(jnp.int16)
        )
    base = len(chunks) * length
    rows = msg_ref.shape[0] - base
    if rows > len(scales):
        scales.append(jnp.zeros((rows - len(scales), length), jnp.float32))
    msg_ref[base:] = jnp.concatenate(scales, axis=0).astype(jnp.int32).astype(jnp.int16)


def spread(msg_ref, ranks, i, base):
    length = msg_ref.shape[1]
    keep = length // GROUPS
    spare = (length - keep) // SUB
    rows = msg_ref[i * length : (i + 1) * length].astype(jnp.int32).astype(jnp.float32)
    tail = msg_ref[base:].astype(jnp.int32).astype(jnp.float32)
    unit = jnp.exp2(tail[i * GROUPS : (i + 1) * GROUPS]) * (1.0 / STEPS)
    out = []
    for g, rank in enumerate(ranks):
        values = rows[g * keep : (g + 1) * keep] * unit[g : g + 1]
        dense = []
        for t in range(length // SUB):
            at = rank[t * SUB : (t + 1) * SUB]
            pieces = {
                p: values[p * SUB : (p + 1) * SUB]
                for p in range(max(0, t - spare), min(keep // SUB - 1, t) + 1)
            }
            dense.append(jnp.where(at >= 0, choose(pieces, at), 0.0))
        out.append(jnp.concatenate(dense, axis=0).T)
    return jnp.concatenate(out, axis=0)


def copy_out(held_ref, out_ref, sem, base, rows):
    place = pl.ds(base + rows.start, rows.stop - rows.start)
    return pltpu.make_async_copy(
        held_ref.at[pl.ds(rows.start, rows.stop - rows.start)], out_ref.at[place], sem
    )


def own_kernel(parts, weights_ref, short_ref, m_ref, g_ref, p_ref, *refs):
    del p_ref
    msgs, refs = refs[: len(parts)], refs[len(parts) :]
    new_ref, back_ref = refs
    length = m_ref.shape[1]
    size = GROUPS * length
    weights = weights_ref[...]
    numbers = short_ref[...].astype(jnp.int32)
    for chunks, msg_ref in zip(parts, msgs):
        for i, c in enumerate(chunks):
            ranks = [
                positions(numbers[:, b * length : (b + 1) * length], length)
                for b in range(c * GROUPS, (c + 1) * GROUPS)
            ]
            rows = slice(c * size, (c + 1) * size)
            back = transform(spread(msg_ref, ranks, i, len(chunks) * length), weights)
            back_ref[rows] = back
            new_ref[rows] = 0.999 * m_ref[rows] + g_ref[rows].astype(jnp.float32) - back


def positions_kernel(others, new_ref, *refs):
    shorts, (new_out_ref, *places, sem) = refs[:others], refs[others:]
    copy = pltpu.make_async_copy(new_ref, new_out_ref, sem.at[0])
    copy.start()
    for short_ref, ranks_ref in zip(shorts, places):
        length, count = ranks_ref.shape
        numbers = short_ref[...].astype(jnp.int32)
        for b in range(count // length):
            lanes = slice(b * length, (b + 1) * length)
            ranks_ref[:, lanes] = positions(numbers[:, lanes], length)
    copy.wait()


def finish_kernel(parts, islands, weights_ref, back_ref, p_ref, *refs):
    msgs, refs = refs[: islands - 1], refs[islands - 1 :]
    places, refs = refs[: islands - 1], refs[islands - 1 :]
    chunks = parts[-1]
    length = p_ref.shape[1]
    size = GROUPS * length
    last = chunks.stop * size == p_ref.shape[0]
    first = chunks.start * size
    copies = []
    if last:
        *earlier, out_ref, held_ref, sems = refs
        for i, (part, early_ref) in enumerate(zip(parts, earlier)):
            rows = slice(0, early_ref.shape[0])
            copies.append(copy_out(early_ref, out_ref, sems.at[i], part.start * size, rows))
            copies[-1].start()
    else:
        (held_ref,) = refs
    weights = weights_ref[...]
    for i, c in enumerate(chunks):
        rows = slice(c * size, (c + 1) * size)
        terms = [back_ref[rows]]
        for msg_ref, ranks_ref in zip(msgs, places):
            ranks = [
                ranks_ref[:, b * length : (b + 1) * length]
                for b in range(c * GROUPS, (c + 1) * GROUPS)
            ]
            kept = spread(msg_ref, ranks, i, len(chunks) * length)
            terms.append(transform(kept, weights))
        if islands == 2:
            total = terms[0] + terms[1]
        else:
            total = None
            for island in range(islands):
                term = terms[0]
                for away in range(1, islands):
                    origin = lax.rem(lax.axis_index("island") + islands - away, islands)
                    term = jnp.where(origin == island, terms[away], term)
                total = term if total is None else total + term
        done = slice(i * size, (i + 1) * size)
        held_ref[done] = (p_ref[rows] - total * (1.0 / islands)).astype(held_ref.dtype)
        if last:
            sem = sems.at[len(parts) - 1 + i]
            copies.append(copy_out(held_ref, out_ref, sem, first, done))
            copies[-1].start()
    for copy in copies:
        copy.wait()


def on_chip(
    kernel, out_shape, *args, name, flops=5 * 10**8, held=None, copies=0, onto={}
):
    vmem = pl.BlockSpec(memory_space=pltpu.VMEM)
    out_specs = [vmem] * len(out_shape)
    scratch = []
    if copies:
        out_specs[0] = pl.BlockSpec(memory_space=pl.ANY)
        scratch = [] if held is None else [pltpu.VMEM(held.shape, held.dtype)]
        scratch.append(pltpu.SemaphoreType.DMA((copies,)))
    return pl.pallas_call(
        kernel,
        in_specs=[vmem] * len(args),
        out_specs=out_specs,
        out_shape=out_shape,
        scratch_shapes=scratch,
        input_output_aliases=onto,
        compiler_params=pltpu.CompilerParams(vmem_limit_bytes=VMEM_LIMIT),
        cost_estimate=pl.CostEstimate(flops=flops, bytes_accessed=flops // 128, transcendentals=0),
        name=name,
    )(*args)


def local(momentum, gradient, params, indices):
    islands = lax.axis_size("island")
    _, count, length = momentum.shape
    numbers = indices[0].T
    chunks = count // (GROUPS * length)
    parts = [part for part in (range(chunks - 2), range(chunks - 2, chunks)) if len(part)]
    rings = [
        [(i, (i + away) % islands) for i in range(islands)] for away in range(1, islands)
    ]

    def array(rows, dtype, lanes=length):
        return jax.ShapeDtypeStruct((rows, lanes), dtype)

    def to_others(x):
        return [lax.ppermute(x, "island", ring) for ring in rings]

    weights = array(2 * length, jnp.bfloat16, 2 * length)
    prepared = [array(chunks * length, jnp.int32), weights, weights]
    short, *early = on_chip(
        shorten_kernel, [array(numbers.shape[0], jnp.int16, count)] + prepared, numbers,
        name="shorten", flops=5 * 10**9,
    )
    other_numbers = to_others(short)
    picks, forward, inverse = on_chip(
        order_kernel, prepared, short, *early,
        name="order", flops=10**4, onto={1: 0, 2: 1, 3: 2},
    )
    msgs = []
    other_msgs = []
    for part in parts:
        tail = -(-(len(part) * GROUPS) // 16) * 16
        (msg,) = on_chip(
            functools.partial(encode_kernel, part),
            [array(len(part) * length + tail, jnp.int16)],
            forward, picks, momentum[0], gradient[0],
            name="encode",
        )
        msgs.append(msg)
        other_msgs.append(to_others(msg))
    wide = array(count, jnp.float32)
    new, back = on_chip(
        functools.partial(own_kernel, parts), [wide, wide],
        inverse, short, momentum[0], gradient[0], params, *msgs,
        name="own",
    )
    new_momentum, *places = on_chip(
        functools.partial(positions_kernel, islands - 1),
        [wide] + [array(length, jnp.int32, count)] * (islands - 1), new, *other_numbers,
        name="positions", copies=1,
    )
    fresh = []
    for i, (part, others) in enumerate(zip(parts, other_msgs)):
        last = i == len(parts) - 1
        mine = array(len(part) * GROUPS * length, jnp.bfloat16)
        (done,) = on_chip(
            functools.partial(finish_kernel, parts[: i + 1], islands),
            [array(count, jnp.bfloat16) if last else mine],
            inverse, back, params, *others, *places, *(fresh if last else []),
            name="finish", held=mine, copies=(i + len(part)) * last,
        )
        fresh.append(done)
    return new_momentum[None], fresh[-1]


def solution(mesh):
    in_specs = (
        P("island", "fsdp", None),
        P("island", "fsdp", None),
        P("fsdp", None),
        P("island", "fsdp", None),
    )
    out_specs = (P("island", "fsdp", None), P("fsdp", None))
    return jax.shard_map(local, mesh=mesh, in_specs=in_specs, out_specs=out_specs, check_vma=False)
```

```python
import functools
import math

import jax
import jax.numpy as jnp
from jax import lax
from jax.experimental import pallas as pl
from jax.experimental.pallas import tpu as pltpu
from jax.sharding import PartitionSpec as P

STEPS = 32000.0
GROUPS = 4
TINY = 1e-30
WORD = 32
SUB = 8
VMEM_LIMIT = 16 * 2**20


def dct_table(length):
    freq = lax.broadcasted_iota(jnp.int32, (length, length), 0)
    place = lax.broadcasted_iota(jnp.int32, (length, length), 1)
    turn = ((2 * place + 1) * freq) & (4 * length - 1)
    x = (jnp.abs(turn - 2 * length) - length).astype(jnp.float32) * (math.pi / (2 * length))
    square = x * x
    series = jnp.full_like(x, 1.0 / math.factorial(15))
    for n in range(13, 0, -2):
        series = 1.0 / math.factorial(n) - square * series
    scale = jnp.where(freq == 0, math.sqrt(1.0 / length), math.sqrt(2.0 / length))
    return scale * (x * series)


def two_parts(x):
    hi = x.astype(jnp.bfloat16)
    return hi, (x - hi.astype(jnp.float32)).astype(jnp.bfloat16)


def weights_of(table):
    hi, lo = two_parts(table)
    return jnp.concatenate(
        [jnp.concatenate([hi, lo], axis=1), jnp.concatenate([hi, jnp.zeros_like(hi)], axis=1)],
        axis=0,
    )


def transform(x, weights):
    both = jnp.dot(
        jnp.concatenate(two_parts(x), axis=1), weights, preferred_element_type=jnp.float32
    )
    length = x.shape[1]
    return both[:, :length] + both[:, length:]


def rows_of(x, index):
    return jnp.take_along_axis(x, index, axis=0, mode="promise_in_bounds")


def row_iota():
    return lax.broadcasted_iota(jnp.int32, (SUB, 128), 0)


def mask_words(part, length):
    rows = [part[v : v + SUB] for v in range(0, part.shape[0], SUB)]
    bits = [lax.shift_left(jnp.ones_like(r), r & (WORD - 1)) for r in rows]
    words = []
    for w in range(length // WORD):
        total = None
        for r, bit in zip(rows, bits):
            term = jnp.where(lax.shift_right_logical(r, 5) == w, bit, 0)
            total = term if total is None else total + term
        for shift in (4, 2, 1):
            total = total + pltpu.roll(total, shift, 0)
        words.append(total)
    return words


def bases_of(words):
    bases = [jnp.zeros_like(words[0])]
    for word in words[:-1]:
        bases.append(bases[-1] + lax.population_count(word))
    return bases


def sorted_numbers(part, length):
    words = mask_words(part, length)
    bases = bases_of(words)
    out = []
    for v in range(0, part.shape[0], SUB):
        rank = row_iota() + v
        word, base, end = words[0], bases[0], jnp.full_like(rank, WORD)
        for w in range(1, len(words)):
            up = rank >= bases[w]
            word = jnp.where(up, words[w], word)
            base = jnp.where(up, bases[w], base)
            end = jnp.where(up, (w + 1) * WORD, end)
        rank = rank - base
        left = jnp.full_like(rank, WORD)
        half = WORD // 2
        while half:
            less = left - half
            below = lax.population_count(lax.shift_left(word, less))
            left = jnp.where(rank >= below, less, left)
            half //= 2
        out.append(end - left)
    return jnp.concatenate(out, axis=0)


def positions(part, length):
    words = mask_words(part, length)
    bases = bases_of(words)
    out = []
    for t in range(0, length, SUB):
        place = row_iota() + t % WORD
        word = words[t // WORD]
        low = lax.shift_left(jnp.ones_like(place), place) - 1
        rank = lax.population_count(word & low) + bases[t // WORD]
        held = lax.shift_right_logical(word, place) & 1
        out.append(jnp.where(held == 1, rank, -1))
    return jnp.concatenate(out, axis=0)


def choose(pieces, index):
    inner = index & (SUB - 1)
    found = {p: rows_of(x, inner) for p, x in pieces.items()}
    bit = SUB
    while len(found) > 1:
        up = (index & bit) != 0
        halves = {}
        for p in sorted({p // 2 for p in found}):
            low, high = found.get(2 * p), found.get(2 * p + 1)
            if low is None or high is None:
                halves[p] = high if low is None else low
            else:
                halves[p] = jnp.where(up, high, low)
        found = halves
        bit *= 2
    return next(iter(found.values()))


def prepare(numbers, picks_ref, forward_ref, inverse_ref):
    length = picks_ref.shape[1]
    table = dct_table(length)
    forward_ref[...] = weights_of(table.T)
    inverse_ref[...] = weights_of(table)
    for c in range(picks_ref.shape[0] // length):
        picks_ref[c * length : (c + 1) * length] = jnp.concatenate(
            [
                sorted_numbers(numbers[:, b * length : (b + 1) * length], length)
                for b in range(c * GROUPS, (c + 1) * GROUPS)
            ],
            axis=0,
        )


def shorten_kernel(idx_ref, short_ref, *prepared):
    short_ref[...] = idx_ref[...].astype(jnp.int16)

    @pl.when(lax.axis_index("island") == 0)
    def _():
        prepare(idx_ref[...], *prepared)


def order_kernel(short_ref, *refs):
    @pl.when(lax.axis_index("island") != 0)
    def _():
        prepare(short_ref[...].astype(jnp.int32), *refs[len(refs) // 2 :])


def encode_kernel(parts, weights_ref, picks_ref, m_ref, g_ref, *msgs):
    length = m_ref.shape[1]
    keep = length // GROUPS
    spare = (length - keep) // SUB
    weights = weights_ref[...]
    for chunks, msg_ref in zip(parts, msgs):
        scales = []
        for i, c in enumerate(chunks):
            rows = slice(c * GROUPS * length, (c + 1) * GROUPS * length)
            mom = 0.999 * m_ref[rows] + g_ref[rows].astype(jnp.float32)
            coef = transform(mom, weights)
            coded = []
            for g in range(GROUPS):
                turned = coef[g * length : (g + 1) * length].T
                values = []
                for v in range(keep // SUB):
                    at = c * length + g * keep + v * SUB
                    pieces = {
                        p: turned[p * SUB : (p + 1) * SUB] for p in range(v, v + spare + 1)
                    }
                    values.append(choose(pieces, picks_ref[at : at + SUB]))
                part = jnp.concatenate(values, axis=0)
                top = jnp.max(jnp.abs(part), axis=0, keepdims=True)
                power = jnp.ceil(jnp.log2(jnp.maximum(top, TINY)))
                scales.append(power)
                coded.append(jnp.round(part * (STEPS * jnp.exp2(-power))))
            msg_ref[i * length : (i + 1) * length] = (
                jnp.concatenate(coded, axis=0).astype(jnp.int32).astype(jnp.int16)
            )
        base = len(chunks) * length
        rows = msg_ref.shape[0] - base
        if rows > len(scales):
            scales.append(jnp.zeros((rows - len(scales), length), jnp.float32))
        msg_ref[base:] = jnp.concatenate(scales, axis=0).astype(jnp.int32).astype(jnp.int16)


def spread(msg_ref, ranks, i, base):
    length = msg_ref.shape[1]
    keep = length // GROUPS
    spare = (length - keep) // SUB
    rows = msg_ref[i * length : (i + 1) * length].astype(jnp.int32).astype(jnp.float32)
    tail = msg_ref[base:].astype(jnp.int32).astype(jnp.float32)
    unit = jnp.exp2(tail[i * GROUPS : (i + 1) * GROUPS]) * (1.0 / STEPS)
    out = []
    for g, rank in enumerate(ranks):
        values = rows[g * keep : (g + 1) * keep] * unit[g : g + 1]
        dense = []
        for t in range(length // SUB):
            at = rank[t * SUB : (t + 1) * SUB]
            pieces = {
                p: values[p * SUB : (p + 1) * SUB]
                for p in range(max(0, t - spare), min(keep // SUB - 1, t) + 1)
            }
            dense.append(jnp.where(at >= 0, choose(pieces, at), 0.0))
        out.append(jnp.concatenate(dense, axis=0).T)
    return jnp.concatenate(out, axis=0)


def copy_out(held_ref, out_ref, sem, base, rows):
    place = pl.ds(base + rows.start, rows.stop - rows.start)
    return pltpu.make_async_copy(
        held_ref.at[pl.ds(rows.start, rows.stop - rows.start)], out_ref.at[place], sem
    )


def own_kernel(parts, weights_ref, short_ref, m_ref, g_ref, p_ref, *refs):
    del p_ref
    msgs, refs = refs[: len(parts)], refs[len(parts) :]
    new_ref, back_ref = refs
    length = m_ref.shape[1]
    size = GROUPS * length
    weights = weights_ref[...]
    numbers = short_ref[...].astype(jnp.int32)
    for chunks, msg_ref in zip(parts, msgs):
        for i, c in enumerate(chunks):
            ranks = [
                positions(numbers[:, b * length : (b + 1) * length], length)
                for b in range(c * GROUPS, (c + 1) * GROUPS)
            ]
            rows = slice(c * size, (c + 1) * size)
            back = transform(spread(msg_ref, ranks, i, len(chunks) * length), weights)
            back_ref[rows] = back
            new_ref[rows] = 0.999 * m_ref[rows] + g_ref[rows].astype(jnp.float32) - back


def positions_kernel(others, new_ref, *refs):
    shorts, (new_out_ref, *places, sem) = refs[:others], refs[others:]
    copy = pltpu.make_async_copy(new_ref, new_out_ref, sem.at[0])
    copy.start()
    for short_ref, ranks_ref in zip(shorts, places):
        length, count = ranks_ref.shape
        numbers = short_ref[...].astype(jnp.int32)
        for b in range(count // length):
            lanes = slice(b * length, (b + 1) * length)
            ranks_ref[:, lanes] = positions(numbers[:, lanes], length)
    copy.wait()


def finish_kernel(parts, islands, weights_ref, back_ref, p_ref, *refs):
    msgs, refs = refs[: islands - 1], refs[islands - 1 :]
    places, refs = refs[: islands - 1], refs[islands - 1 :]
    chunks = parts[-1]
    length = p_ref.shape[1]
    size = GROUPS * length
    last = chunks.stop * size == p_ref.shape[0]
    first = chunks.start * size
    copies = []
    if last:
        *earlier, out_ref, held_ref, sems = refs
        for i, (part, early_ref) in enumerate(zip(parts, earlier)):
            rows = slice(0, early_ref.shape[0])
            copies.append(copy_out(early_ref, out_ref, sems.at[i], part.start * size, rows))
            copies[-1].start()
    else:
        (held_ref,) = refs
    weights = weights_ref[...]
    for i, c in enumerate(chunks):
        rows = slice(c * size, (c + 1) * size)
        terms = [back_ref[rows]]
        for msg_ref, ranks_ref in zip(msgs, places):
            ranks = [
                ranks_ref[:, b * length : (b + 1) * length]
                for b in range(c * GROUPS, (c + 1) * GROUPS)
            ]
            kept = spread(msg_ref, ranks, i, len(chunks) * length)
            terms.append(transform(kept, weights))
        if islands == 2:
            total = terms[0] + terms[1]
        else:
            total = None
            for island in range(islands):
                term = terms[0]
                for away in range(1, islands):
                    origin = lax.rem(lax.axis_index("island") + islands - away, islands)
                    term = jnp.where(origin == island, terms[away], term)
                total = term if total is None else total + term
        done = slice(i * size, (i + 1) * size)
        held_ref[done] = (p_ref[rows] - total * (1.0 / islands)).astype(held_ref.dtype)
        if last:
            sem = sems.at[len(parts) - 1 + i]
            copies.append(copy_out(held_ref, out_ref, sem, first, done))
            copies[-1].start()
    for copy in copies:
        copy.wait()


def on_chip(
    kernel, out_shape, *args, name, flops=5 * 10**8, held=None, copies=0, onto={}
):
    vmem = pl.BlockSpec(memory_space=pltpu.VMEM)
    out_specs = [vmem] * len(out_shape)
    scratch = []
    if copies:
        out_specs[0] = pl.BlockSpec(memory_space=pl.ANY)
        scratch = [] if held is None else [pltpu.VMEM(held.shape, held.dtype)]
        scratch.append(pltpu.SemaphoreType.DMA((copies,)))
    return pl.pallas_call(
        kernel,
        in_specs=[vmem] * len(args),
        out_specs=out_specs,
        out_shape=out_shape,
        scratch_shapes=scratch,
        input_output_aliases=onto,
        compiler_params=pltpu.CompilerParams(vmem_limit_bytes=VMEM_LIMIT),
        cost_estimate=pl.CostEstimate(flops=flops, bytes_accessed=flops // 128, transcendentals=0),
        name=name,
    )(*args)


def local(momentum, gradient, params, indices):
    islands = lax.axis_size("island")
    _, count, length = momentum.shape
    numbers = indices[0].T
    chunks = count // (GROUPS * length)
    parts = [part for part in (range(chunks - 2), range(chunks - 2, chunks)) if len(part)]
    rings = [
        [(i, (i + away) % islands) for i in range(islands)] for away in range(1, islands)
    ]

    def array(rows, dtype, lanes=length):
        return jax.ShapeDtypeStruct((rows, lanes), dtype)

    def to_others(x):
        return [lax.ppermute(x, "island", ring) for ring in rings]

    weights = array(2 * length, jnp.bfloat16, 2 * length)
    prepared = [array(chunks * length, jnp.int32), weights, weights]
    short, *early = on_chip(
        shorten_kernel, [array(numbers.shape[0], jnp.int16, count)] + prepared, numbers,
        name="shorten", flops=5 * 10**9,
    )
    other_numbers = to_others(short)
    picks, forward, inverse = on_chip(
        order_kernel, prepared, short, *early,
        name="order", flops=10**4, onto={1: 0, 2: 1, 3: 2},
    )
    tails = [-(-(len(part) * GROUPS) // 16) * 16 for part in parts]
    msgs = on_chip(
        functools.partial(encode_kernel, parts),
        [array(len(part) * length + tail, jnp.int16) for part, tail in zip(parts, tails)],
        forward, picks, momentum[0], gradient[0],
        name="encode",
    )
    other_msgs = [to_others(msg) for msg in msgs]
    wide = array(count, jnp.float32)
    new, back = on_chip(
        functools.partial(own_kernel, parts), [wide, wide],
        inverse, short, momentum[0], gradient[0], params, *msgs,
        name="own",
    )
    new_momentum, *places = on_chip(
        functools.partial(positions_kernel, islands - 1),
        [wide] + [array(length, jnp.int32, count)] * (islands - 1), new, *other_numbers,
        name="positions", copies=1,
    )
    fresh = []
    for i, (part, others) in enumerate(zip(parts, other_msgs)):
        last = i == len(parts) - 1
        mine = array(len(part) * GROUPS * length, jnp.bfloat16)
        (done,) = on_chip(
            functools.partial(finish_kernel, parts[: i + 1], islands),
            [array(count, jnp.bfloat16) if last else mine],
            inverse, back, params, *others, *places, *(fresh if last else []),
            name="finish", held=mine, copies=(i + len(part)) * last,
        )
        fresh.append(done)
    return new_momentum[None], fresh[-1]


def solution(mesh):
    in_specs = (
        P("island", "fsdp", None),
        P("island", "fsdp", None),
        P("fsdp", None),
        P("island", "fsdp", None),
    )
    out_specs = (P("island", "fsdp", None), P("fsdp", None))
    return jax.shard_map(local, mesh=mesh, in_specs=in_specs, out_specs=out_specs, check_vma=False)
```

```python
import functools
import math

import jax
import jax.numpy as jnp
from jax import lax
from jax.experimental import pallas as pl
from jax.experimental.pallas import tpu as pltpu
from jax.sharding import PartitionSpec as P

STEPS = 32000.0
GROUPS = 4
TINY = 1e-30
WORD = 32
SUB = 8
VMEM_LIMIT = 16 * 2**20


def dct_table(length):
    freq = lax.broadcasted_iota(jnp.int32, (length, length), 0)
    place = lax.broadcasted_iota(jnp.int32, (length, length), 1)
    turn = ((2 * place + 1) * freq) & (4 * length - 1)
    x = (jnp.abs(turn - 2 * length) - length).astype(jnp.float32) * (math.pi / (2 * length))
    square = x * x
    series = jnp.full_like(x, 1.0 / math.factorial(15))
    for n in range(13, 0, -2):
        series = 1.0 / math.factorial(n) - square * series
    scale = jnp.where(freq == 0, math.sqrt(1.0 / length), math.sqrt(2.0 / length))
    return scale * (x * series)


def two_parts(x):
    hi = x.astype(jnp.bfloat16)
    return hi, (x - hi.astype(jnp.float32)).astype(jnp.bfloat16)


def weights_of(table):
    hi, lo = two_parts(table)
    return jnp.concatenate(
        [jnp.concatenate([hi, lo], axis=1), jnp.concatenate([hi, jnp.zeros_like(hi)], axis=1)],
        axis=0,
    )


def transform(x, weights):
    both = jnp.dot(
        jnp.concatenate(two_parts(x), axis=1), weights, preferred_element_type=jnp.float32
    )
    length = x.shape[1]
    return both[:, :length] + both[:, length:]


def rows_of(x, index):
    return jnp.take_along_axis(x, index, axis=0, mode="promise_in_bounds")


def row_iota():
    return lax.broadcasted_iota(jnp.int32, (SUB, 128), 0)


def mask_words(part, length):
    rows = [part[v : v + SUB] for v in range(0, part.shape[0], SUB)]
    bits = [lax.shift_left(jnp.ones_like(r), r & (WORD - 1)) for r in rows]
    words = []
    for w in range(length // WORD):
        total = None
        for r, bit in zip(rows, bits):
            term = jnp.where(lax.shift_right_logical(r, 5) == w, bit, 0)
            total = term if total is None else total + term
        for shift in (4, 2, 1):
            total = total + pltpu.roll(total, shift, 0)
        words.append(total)
    return words


def bases_of(words):
    bases = [jnp.zeros_like(words[0])]
    for word in words[:-1]:
        bases.append(bases[-1] + lax.population_count(word))
    return bases


def sorted_numbers(part, length):
    words = mask_words(part, length)
    bases = bases_of(words)
    out = []
    for v in range(0, part.shape[0], SUB):
        rank = row_iota() + v
        word, base, end = words[0], bases[0], jnp.full_like(rank, WORD)
        for w in range(1, len(words)):
            up = rank >= bases[w]
            word = jnp.where(up, words[w], word)
            base = jnp.where(up, bases[w], base)
            end = jnp.where(up, (w + 1) * WORD, end)
        rank = rank - base
        left = jnp.full_like(rank, WORD)
        half = WORD // 2
        while half:
            less = left - half
            below = lax.population_count(lax.shift_left(word, less))
            left = jnp.where(rank >= below, less, left)
            half //= 2
        out.append(end - left)
    return jnp.concatenate(out, axis=0)


def positions(part, length):
    words = mask_words(part, length)
    bases = bases_of(words)
    out = []
    for t in range(0, length, SUB):
        place = row_iota() + t % WORD
        word = words[t // WORD]
        low = lax.shift_left(jnp.ones_like(place), place) - 1
        rank = lax.population_count(word & low) + bases[t // WORD]
        held = lax.shift_right_logical(word, place) & 1
        out.append(jnp.where(held == 1, rank, -1))
    return jnp.concatenate(out, axis=0)


def choose(pieces, index):
    inner = index & (SUB - 1)
    found = {p: rows_of(x, inner) for p, x in pieces.items()}
    bit = SUB
    while len(found) > 1:
        up = (index & bit) != 0
        halves = {}
        for p in sorted({p // 2 for p in found}):
            low, high = found.get(2 * p), found.get(2 * p + 1)
            if low is None or high is None:
                halves[p] = high if low is None else low
            else:
                halves[p] = jnp.where(up, high, low)
        found = halves
        bit *= 2
    return next(iter(found.values()))


def prepare(numbers, picks_ref, forward_ref, inverse_ref):
    length = picks_ref.shape[1]
    table = dct_table(length)
    forward_ref[...] = weights_of(table.T)
    inverse_ref[...] = weights_of(table)
    for c in range(picks_ref.shape[0] // length):
        picks_ref[c * length : (c + 1) * length] = jnp.concatenate(
            [
                sorted_numbers(numbers[:, b * length : (b + 1) * length], length)
                for b in range(c * GROUPS, (c + 1) * GROUPS)
            ],
            axis=0,
        )


def shorten_kernel(idx_ref, short_ref, *prepared):
    short_ref[...] = idx_ref[...].astype(jnp.int16)

    @pl.when(lax.axis_index("island") == 0)
    def _():
        prepare(idx_ref[...], *prepared)


def order_kernel(short_ref, *refs):
    @pl.when(lax.axis_index("island") != 0)
    def _():
        prepare(short_ref[...].astype(jnp.int32), *refs[len(refs) // 2 :])


def encode_kernel(parts, weights_ref, picks_ref, m_ref, g_ref, *msgs):
    length = m_ref.shape[1]
    keep = length // GROUPS
    spare = (length - keep) // SUB
    weights = weights_ref[...]
    scales = []
    for chunks, msg_ref in zip(parts, msgs):
        for i, c in enumerate(chunks):
            rows = slice(c * GROUPS * length, (c + 1) * GROUPS * length)
            mom = 0.999 * m_ref[rows] + g_ref[rows].astype(jnp.float32)
            coef = transform(mom, weights)
            coded = []
            for g in range(GROUPS):
                turned = coef[g * length : (g + 1) * length].T
                values = []
                for v in range(keep // SUB):
                    at = c * length + g * keep + v * SUB
                    pieces = {
                        p: turned[p * SUB : (p + 1) * SUB] for p in range(v, v + spare + 1)
                    }
                    values.append(choose(pieces, picks_ref[at : at + SUB]))
                part = jnp.concatenate(values, axis=0)
                top = jnp.max(jnp.abs(part), axis=0, keepdims=True)
                power = jnp.ceil(jnp.log2(jnp.maximum(top, TINY)))
                scales.append(power)
                coded.append(jnp.round(part * (STEPS * jnp.exp2(-power))))
            msg_ref[i * length : (i + 1) * length] = (
                jnp.concatenate(coded, axis=0).astype(jnp.int32).astype(jnp.int16)
            )
    base = len(parts[0]) * length
    rows = msgs[0].shape[0] - base
    if rows > len(scales):
        scales.append(jnp.zeros((rows - len(scales), length), jnp.float32))
    msgs[0][base:] = jnp.concatenate(scales, axis=0).astype(jnp.int32).astype(jnp.int16)


def spread(msg_ref, first_ref, ranks, i, scales):
    length = msg_ref.shape[1]
    keep = length // GROUPS
    spare = (length - keep) // SUB
    rows = msg_ref[i * length : (i + 1) * length].astype(jnp.int32).astype(jnp.float32)
    base = scales // 16 * 16
    tail = first_ref[base : base + 16].astype(jnp.int32).astype(jnp.float32)
    unit = jnp.exp2(tail[scales - base : scales - base + GROUPS]) * (1.0 / STEPS)
    out = []
    for g, rank in enumerate(ranks):
        values = rows[g * keep : (g + 1) * keep] * unit[g : g + 1]
        dense = []
        for t in range(length // SUB):
            at = rank[t * SUB : (t + 1) * SUB]
            pieces = {
                p: values[p * SUB : (p + 1) * SUB]
                for p in range(max(0, t - spare), min(keep // SUB - 1, t) + 1)
            }
            dense.append(jnp.where(at >= 0, choose(pieces, at), 0.0))
        out.append(jnp.concatenate(dense, axis=0).T)
    return jnp.concatenate(out, axis=0)


def copy_out(held_ref, out_ref, sem, base, rows):
    place = pl.ds(base + rows.start, rows.stop - rows.start)
    return pltpu.make_async_copy(
        held_ref.at[pl.ds(rows.start, rows.stop - rows.start)], out_ref.at[place], sem
    )


def own_kernel(parts, weights_ref, short_ref, m_ref, g_ref, p_ref, *refs):
    del p_ref
    msgs, refs = refs[: len(parts)], refs[len(parts) :]
    new_ref, back_ref = refs
    length = m_ref.shape[1]
    size = GROUPS * length
    weights = weights_ref[...]
    numbers = short_ref[...].astype(jnp.int32)
    for chunks, msg_ref in zip(parts, msgs):
        for i, c in enumerate(chunks):
            ranks = [
                positions(numbers[:, b * length : (b + 1) * length], length)
                for b in range(c * GROUPS, (c + 1) * GROUPS)
            ]
            rows = slice(c * size, (c + 1) * size)
            scales = len(parts[0]) * length + c * GROUPS
            back = transform(spread(msg_ref, msgs[0], ranks, i, scales), weights)
            back_ref[rows] = back
            new_ref[rows] = 0.999 * m_ref[rows] + g_ref[rows].astype(jnp.float32) - back


def positions_kernel(others, new_ref, *refs):
    shorts, (new_out_ref, *places, sem) = refs[:others], refs[others:]
    copy = pltpu.make_async_copy(new_ref, new_out_ref, sem.at[0])
    copy.start()
    for short_ref, ranks_ref in zip(shorts, places):
        length, count = ranks_ref.shape
        numbers = short_ref[...].astype(jnp.int32)
        for b in range(count // length):
            lanes = slice(b * length, (b + 1) * length)
            ranks_ref[:, lanes] = positions(numbers[:, lanes], length)
    copy.wait()


def finish_kernel(parts, islands, weights_ref, back_ref, p_ref, *refs):
    msgs, refs = refs[: islands - 1], refs[islands - 1 :]
    firsts, refs = refs[: islands - 1], refs[islands - 1 :]
    places, refs = refs[: islands - 1], refs[islands - 1 :]
    chunks = parts[-1]
    length = p_ref.shape[1]
    size = GROUPS * length
    last = chunks.stop * size == p_ref.shape[0]
    first = chunks.start * size
    copies = []
    if last:
        *earlier, out_ref, held_ref, sems = refs
        for i, (part, early_ref) in enumerate(zip(parts, earlier)):
            rows = slice(0, early_ref.shape[0])
            copies.append(copy_out(early_ref, out_ref, sems.at[i], part.start * size, rows))
            copies[-1].start()
    else:
        (held_ref,) = refs
    weights = weights_ref[...]
    for i, c in enumerate(chunks):
        rows = slice(c * size, (c + 1) * size)
        terms = [back_ref[rows]]
        for msg_ref, first_ref, ranks_ref in zip(msgs, firsts, places):
            ranks = [
                ranks_ref[:, b * length : (b + 1) * length]
                for b in range(c * GROUPS, (c + 1) * GROUPS)
            ]
            kept = spread(msg_ref, first_ref, ranks, i, len(parts[0]) * length + c * GROUPS)
            terms.append(transform(kept, weights))
        if islands == 2:
            total = terms[0] + terms[1]
        else:
            total = None
            for island in range(islands):
                term = terms[0]
                for away in range(1, islands):
                    origin = lax.rem(lax.axis_index("island") + islands - away, islands)
                    term = jnp.where(origin == island, terms[away], term)
                total = term if total is None else total + term
        done = slice(i * size, (i + 1) * size)
        held_ref[done] = (p_ref[rows] - total * (1.0 / islands)).astype(held_ref.dtype)
        if last:
            sem = sems.at[len(parts) - 1 + i]
            copies.append(copy_out(held_ref, out_ref, sem, first, done))
            copies[-1].start()
    for copy in copies:
        copy.wait()


def on_chip(
    kernel, out_shape, *args, name, flops=5 * 10**8, held=None, copies=0, onto={}
):
    vmem = pl.BlockSpec(memory_space=pltpu.VMEM)
    out_specs = [vmem] * len(out_shape)
    scratch = []
    if copies:
        out_specs[0] = pl.BlockSpec(memory_space=pl.ANY)
        scratch = [] if held is None else [pltpu.VMEM(held.shape, held.dtype)]
        scratch.append(pltpu.SemaphoreType.DMA((copies,)))
    return pl.pallas_call(
        kernel,
        in_specs=[vmem] * len(args),
        out_specs=out_specs,
        out_shape=out_shape,
        scratch_shapes=scratch,
        input_output_aliases=onto,
        compiler_params=pltpu.CompilerParams(vmem_limit_bytes=VMEM_LIMIT),
        cost_estimate=pl.CostEstimate(flops=flops, bytes_accessed=flops // 128, transcendentals=0),
        name=name,
    )(*args)


def local(momentum, gradient, params, indices):
    islands = lax.axis_size("island")
    _, count, length = momentum.shape
    numbers = indices[0].T
    chunks = count // (GROUPS * length)
    parts = [part for part in (range(chunks - 1), range(chunks - 1, chunks)) if len(part)]
    rings = [
        [(i, (i + away) % islands) for i in range(islands)] for away in range(1, islands)
    ]

    def array(rows, dtype, lanes=length):
        return jax.ShapeDtypeStruct((rows, lanes), dtype)

    def to_others(x):
        return [lax.ppermute(x, "island", ring) for ring in rings]

    weights = array(2 * length, jnp.bfloat16, 2 * length)
    prepared = [array(chunks * length, jnp.int32), weights, weights]
    short, *early = on_chip(
        shorten_kernel, [array(numbers.shape[0], jnp.int16, count)] + prepared, numbers,
        name="shorten", flops=5 * 10**9,
    )
    other_numbers = to_others(short)
    picks, forward, inverse = on_chip(
        order_kernel, prepared, short, *early,
        name="order", flops=10**4, onto={1: 0, 2: 1, 3: 2},
    )
    tails = [-(-(chunks * GROUPS) // 16) * 16] + [0] * (len(parts) - 1)
    msgs = on_chip(
        functools.partial(encode_kernel, parts),
        [array(len(part) * length + tail, jnp.int16) for part, tail in zip(parts, tails)],
        forward, picks, momentum[0], gradient[0],
        name="encode",
    )
    other_msgs = [to_others(msg) for msg in msgs]
    wide = array(count, jnp.float32)
    new, back = on_chip(
        functools.partial(own_kernel, parts), [wide, wide],
        inverse, short, momentum[0], gradient[0], params, *msgs,
        name="own",
    )
    new_momentum, *places = on_chip(
        functools.partial(positions_kernel, islands - 1),
        [wide] + [array(length, jnp.int32, count)] * (islands - 1), new, *other_numbers,
        name="positions", copies=1,
    )
    fresh = []
    for i, (part, others) in enumerate(zip(parts, other_msgs)):
        last = i == len(parts) - 1
        mine = array(len(part) * GROUPS * length, jnp.bfloat16)
        (done,) = on_chip(
            functools.partial(finish_kernel, parts[: i + 1], islands),
            [array(count, jnp.bfloat16) if last else mine],
            inverse, back, params, *others, *other_msgs[0], *places, *(fresh if last else []),
            name="finish", held=mine, copies=(i + len(part)) * last,
        )
        fresh.append(done)
    return new_momentum[None], fresh[-1]


def solution(mesh):
    in_specs = (
        P("island", "fsdp", None),
        P("island", "fsdp", None),
        P("fsdp", None),
        P("island", "fsdp", None),
    )
    out_specs = (P("island", "fsdp", None), P("fsdp", None))
    return jax.shard_map(local, mesh=mesh, in_specs=in_specs, out_specs=out_specs, check_vma=False)
```

```python
import functools
import math

import jax
import jax.numpy as jnp
from jax import lax
from jax.experimental import pallas as pl
from jax.experimental.pallas import tpu as pltpu
from jax.sharding import PartitionSpec as P

STEPS = 32000.0
GROUPS = 4
TINY = 1e-30
WORD = 32
SUB = 8
VMEM_LIMIT = 16 * 2**20


def dct_table(length):
    freq = lax.broadcasted_iota(jnp.int32, (length, length), 0)
    place = lax.broadcasted_iota(jnp.int32, (length, length), 1)
    turn = ((2 * place + 1) * freq) & (4 * length - 1)
    x = (jnp.abs(turn - 2 * length) - length).astype(jnp.float32) * (math.pi / (2 * length))
    square = x * x
    series = jnp.full_like(x, 1.0 / math.factorial(15))
    for n in range(13, 0, -2):
        series = 1.0 / math.factorial(n) - square * series
    scale = jnp.where(freq == 0, math.sqrt(1.0 / length), math.sqrt(2.0 / length))
    return scale * (x * series)


def two_parts(x):
    hi = x.astype(jnp.bfloat16)
    return hi, (x - hi.astype(jnp.float32)).astype(jnp.bfloat16)


def weights_of(table):
    hi, lo = two_parts(table)
    return jnp.concatenate([hi, hi, lo], axis=0)


def transform(x, weights):
    hi, lo = two_parts(x)
    return jnp.dot(
        jnp.concatenate([hi, lo, hi], axis=1), weights, preferred_element_type=jnp.float32
    )


def rows_of(x, index):
    return jnp.take_along_axis(x, index, axis=0, mode="promise_in_bounds")


def row_iota():
    return lax.broadcasted_iota(jnp.int32, (SUB, 128), 0)


def mask_words(part, length):
    rows = [part[v : v + SUB] for v in range(0, part.shape[0], SUB)]
    bits = [lax.shift_left(jnp.ones_like(r), r & (WORD - 1)) for r in rows]
    words = []
    for w in range(length // WORD):
        total = None
        for r, bit in zip(rows, bits):
            term = jnp.where(lax.shift_right_logical(r, 5) == w, bit, 0)
            total = term if total is None else total + term
        for shift in (4, 2, 1):
            total = total + pltpu.roll(total, shift, 0)
        words.append(total)
    return words


def bases_of(words):
    bases = [jnp.zeros_like(words[0])]
    for word in words[:-1]:
        bases.append(bases[-1] + lax.population_count(word))
    return bases


def sorted_numbers(part, length):
    words = mask_words(part, length)
    bases = bases_of(words)
    out = []
    for v in range(0, part.shape[0], SUB):
        rank = row_iota() + v
        word, base, end = words[0], bases[0], jnp.full_like(rank, WORD)
        for w in range(1, len(words)):
            up = rank >= bases[w]
            word = jnp.where(up, words[w], word)
            base = jnp.where(up, bases[w], base)
            end = jnp.where(up, (w + 1) * WORD, end)
        rank = rank - base
        left = jnp.full_like(rank, WORD)
        half = WORD // 2
        while half:
            less = left - half
            below = lax.population_count(lax.shift_left(word, less))
            left = jnp.where(rank >= below, less, left)
            half //= 2
        out.append(end - left)
    return jnp.concatenate(out, axis=0)


def positions(part, length):
    words = mask_words(part, length)
    bases = bases_of(words)
    out = []
    for t in range(0, length, SUB):
        place = row_iota() + t % WORD
        word = words[t // WORD]
        low = lax.shift_left(jnp.ones_like(place), place) - 1
        rank = lax.population_count(word & low) + bases[t // WORD]
        held = lax.shift_right_logical(word, place) & 1
        out.append(jnp.where(held == 1, rank, -1))
    return jnp.concatenate(out, axis=0)


def choose(pieces, index):
    inner = index & (SUB - 1)
    found = {p: rows_of(x, inner) for p, x in pieces.items()}
    bit = SUB
    while len(found) > 1:
        up = (index & bit) != 0
        halves = {}
        for p in sorted({p // 2 for p in found}):
            low, high = found.get(2 * p), found.get(2 * p + 1)
            if low is None or high is None:
                halves[p] = high if low is None else low
            else:
                halves[p] = jnp.where(up, high, low)
        found = halves
        bit *= 2
    return next(iter(found.values()))


def prepare(numbers, picks_ref, forward_ref, inverse_ref):
    length = picks_ref.shape[1]
    table = dct_table(length)
    forward_ref[...] = weights_of(table.T)
    inverse_ref[...] = weights_of(table)
    for c in range(picks_ref.shape[0] // length):
        picks_ref[c * length : (c + 1) * length] = jnp.concatenate(
            [
                sorted_numbers(numbers[:, b * length : (b + 1) * length], length)
                for b in range(c * GROUPS, (c + 1) * GROUPS)
            ],
            axis=0,
        )


def shorten_kernel(idx_ref, short_ref, *prepared):
    short_ref[...] = idx_ref[...].astype(jnp.int16)

    @pl.when(lax.axis_index("island") == 0)
    def _():
        prepare(idx_ref[...], *prepared)


def order_kernel(short_ref, *refs):
    @pl.when(lax.axis_index("island") != 0)
    def _():
        prepare(short_ref[...].astype(jnp.int32), *refs[len(refs) // 2 :])


def encode_kernel(parts, weights_ref, picks_ref, m_ref, g_ref, *msgs):
    length = m_ref.shape[1]
    keep = length // GROUPS
    spare = (length - keep) // SUB
    weights = weights_ref[...]
    for chunks, msg_ref in zip(parts, msgs):
        scales = []
        for i, c in enumerate(chunks):
            rows = slice(c * GROUPS * length, (c + 1) * GROUPS * length)
            mom = 0.999 * m_ref[rows] + g_ref[rows].astype(jnp.float32)
            coef = transform(mom, weights)
            coded = []
            for g in range(GROUPS):
                turned = coef[g * length : (g + 1) * length].T
                values = []
                for v in range(keep // SUB):
                    at = c * length + g * keep + v * SUB
                    pieces = {
                        p: turned[p * SUB : (p + 1) * SUB] for p in range(v, v + spare + 1)
                    }
                    values.append(choose(pieces, picks_ref[at : at + SUB]))
                part = jnp.concatenate(values, axis=0)
                top = jnp.max(jnp.abs(part), axis=0, keepdims=True)
                power = jnp.ceil(jnp.log2(jnp.maximum(top, TINY)))
                scales.append(power)
                coded.append(jnp.round(part * (STEPS * jnp.exp2(-power))))
            msg_ref[i * length : (i + 1) * length] = (
                jnp.concatenate(coded, axis=0).astype(jnp.int32).astype(jnp.int16)
            )
        base = len(chunks) * length
        rows = msg_ref.shape[0] - base
        if rows > len(scales):
            scales.append(jnp.zeros((rows - len(scales), length), jnp.float32))
        msg_ref[base:] = jnp.concatenate(scales, axis=0).astype(jnp.int32).astype(jnp.int16)


def spread(msg_ref, ranks, i, base):
    length = msg_ref.shape[1]
    keep = length // GROUPS
    spare = (length - keep) // SUB
    rows = msg_ref[i * length : (i + 1) * length].astype(jnp.int32).astype(jnp.float32)
    tail = msg_ref[base:].astype(jnp.int32).astype(jnp.float32)
    unit = jnp.exp2(tail[i * GROUPS : (i + 1) * GROUPS]) * (1.0 / STEPS)
    out = []
    for g, rank in enumerate(ranks):
        values = rows[g * keep : (g + 1) * keep] * unit[g : g + 1]
        dense = []
        for t in range(length // SUB):
            at = rank[t * SUB : (t + 1) * SUB]
            pieces = {
                p: values[p * SUB : (p + 1) * SUB]
                for p in range(max(0, t - spare), min(keep // SUB - 1, t) + 1)
            }
            dense.append(jnp.where(at >= 0, choose(pieces, at), 0.0))
        out.append(jnp.concatenate(dense, axis=0).T)
    return jnp.concatenate(out, axis=0)


def copy_out(held_ref, out_ref, sem, base, rows):
    place = pl.ds(base + rows.start, rows.stop - rows.start)
    return pltpu.make_async_copy(
        held_ref.at[pl.ds(rows.start, rows.stop - rows.start)], out_ref.at[place], sem
    )


def own_kernel(parts, weights_ref, short_ref, m_ref, g_ref, p_ref, *refs):
    del p_ref
    msgs, refs = refs[: len(parts)], refs[len(parts) :]
    new_ref, back_ref = refs
    length = m_ref.shape[1]
    size = GROUPS * length
    weights = weights_ref[...]
    numbers = short_ref[...].astype(jnp.int32)
    for chunks, msg_ref in zip(parts, msgs):
        for i, c in enumerate(chunks):
            ranks = [
                positions(numbers[:, b * length : (b + 1) * length], length)
                for b in range(c * GROUPS, (c + 1) * GROUPS)
            ]
            rows = slice(c * size, (c + 1) * size)
            back = transform(spread(msg_ref, ranks, i, len(chunks) * length), weights)
            back_ref[rows] = back
            new_ref[rows] = 0.999 * m_ref[rows] + g_ref[rows].astype(jnp.float32) - back


def positions_kernel(others, new_ref, *refs):
    shorts, (new_out_ref, *places, sem) = refs[:others], refs[others:]
    copy = pltpu.make_async_copy(new_ref, new_out_ref, sem.at[0])
    copy.start()
    for short_ref, ranks_ref in zip(shorts, places):
        length, count = ranks_ref.shape
        numbers = short_ref[...].astype(jnp.int32)
        for b in range(count // length):
            lanes = slice(b * length, (b + 1) * length)
            ranks_ref[:, lanes] = positions(numbers[:, lanes], length)
    copy.wait()


def finish_kernel(parts, islands, weights_ref, back_ref, p_ref, *refs):
    msgs, refs = refs[: islands - 1], refs[islands - 1 :]
    places, refs = refs[: islands - 1], refs[islands - 1 :]
    chunks = parts[-1]
    length = p_ref.shape[1]
    size = GROUPS * length
    last = chunks.stop * size == p_ref.shape[0]
    first = chunks.start * size
    copies = []
    if last:
        *earlier, out_ref, held_ref, sems = refs
        for i, (part, early_ref) in enumerate(zip(parts, earlier)):
            rows = slice(0, early_ref.shape[0])
            copies.append(copy_out(early_ref, out_ref, sems.at[i], part.start * size, rows))
            copies[-1].start()
    else:
        (held_ref,) = refs
    weights = weights_ref[...]
    for i, c in enumerate(chunks):
        rows = slice(c * size, (c + 1) * size)
        terms = [back_ref[rows]]
        for msg_ref, ranks_ref in zip(msgs, places):
            ranks = [
                ranks_ref[:, b * length : (b + 1) * length]
                for b in range(c * GROUPS, (c + 1) * GROUPS)
            ]
            kept = spread(msg_ref, ranks, i, len(chunks) * length)
            terms.append(transform(kept, weights))
        if islands == 2:
            total = terms[0] + terms[1]
        else:
            total = None
            for island in range(islands):
                term = terms[0]
                for away in range(1, islands):
                    origin = lax.rem(lax.axis_index("island") + islands - away, islands)
                    term = jnp.where(origin == island, terms[away], term)
                total = term if total is None else total + term
        done = slice(i * size, (i + 1) * size)
        held_ref[done] = (p_ref[rows] - total * (1.0 / islands)).astype(held_ref.dtype)
        if last:
            sem = sems.at[len(parts) - 1 + i]
            copies.append(copy_out(held_ref, out_ref, sem, first, done))
            copies[-1].start()
    for copy in copies:
        copy.wait()


def on_chip(
    kernel, out_shape, *args, name, flops=5 * 10**8, held=None, copies=0, onto={}
):
    vmem = pl.BlockSpec(memory_space=pltpu.VMEM)
    out_specs = [vmem] * len(out_shape)
    scratch = []
    if copies:
        out_specs[0] = pl.BlockSpec(memory_space=pl.ANY)
        scratch = [] if held is None else [pltpu.VMEM(held.shape, held.dtype)]
        scratch.append(pltpu.SemaphoreType.DMA((copies,)))
    return pl.pallas_call(
        kernel,
        in_specs=[vmem] * len(args),
        out_specs=out_specs,
        out_shape=out_shape,
        scratch_shapes=scratch,
        input_output_aliases=onto,
        compiler_params=pltpu.CompilerParams(vmem_limit_bytes=VMEM_LIMIT),
        cost_estimate=pl.CostEstimate(flops=flops, bytes_accessed=flops // 128, transcendentals=0),
        name=name,
    )(*args)


def local(momentum, gradient, params, indices):
    islands = lax.axis_size("island")
    _, count, length = momentum.shape
    numbers = indices[0].T
    chunks = count // (GROUPS * length)
    parts = [part for part in (range(chunks - 2), range(chunks - 2, chunks)) if len(part)]
    rings = [
        [(i, (i + away) % islands) for i in range(islands)] for away in range(1, islands)
    ]

    def array(rows, dtype, lanes=length):
        return jax.ShapeDtypeStruct((rows, lanes), dtype)

    def to_others(x):
        return [lax.ppermute(x, "island", ring) for ring in rings]

    weights = array(3 * length, jnp.bfloat16)
    prepared = [array(chunks * length, jnp.int32), weights, weights]
    short, *early = on_chip(
        shorten_kernel, [array(numbers.shape[0], jnp.int16, count)] + prepared, numbers,
        name="shorten", flops=5 * 10**9,
    )
    other_numbers = to_others(short)
    picks, forward, inverse = on_chip(
        order_kernel, prepared, short, *early,
        name="order", flops=10**4, onto={1: 0, 2: 1, 3: 2},
    )
    tails = [-(-(len(part) * GROUPS) // 16) * 16 for part in parts]
    msgs = on_chip(
        functools.partial(encode_kernel, parts),
        [array(len(part) * length + tail, jnp.int16) for part, tail in zip(parts, tails)],
        forward, picks, momentum[0], gradient[0],
        name="encode",
    )
    other_msgs = [to_others(msg) for msg in msgs]
    wide = array(count, jnp.float32)
    new, back = on_chip(
        functools.partial(own_kernel, parts), [wide, wide],
        inverse, short, momentum[0], gradient[0], params, *msgs,
        name="own",
    )
    new_momentum, *places = on_chip(
        functools.partial(positions_kernel, islands - 1),
        [wide] + [array(length, jnp.int32, count)] * (islands - 1), new, *other_numbers,
        name="positions", copies=1,
    )
    fresh = []
    for i, (part, others) in enumerate(zip(parts, other_msgs)):
        last = i == len(parts) - 1
        mine = array(len(part) * GROUPS * length, jnp.bfloat16)
        (done,) = on_chip(
            functools.partial(finish_kernel, parts[: i + 1], islands),
            [array(count, jnp.bfloat16) if last else mine],
            inverse, back, params, *others, *places, *(fresh if last else []),
            name="finish", held=mine, copies=(i + len(part)) * last,
        )
        fresh.append(done)
    return new_momentum[None], fresh[-1]


def solution(mesh):
    in_specs = (
        P("island", "fsdp", None),
        P("island", "fsdp", None),
        P("fsdp", None),
        P("island", "fsdp", None),
    )
    out_specs = (P("island", "fsdp", None), P("fsdp", None))
    return jax.shard_map(local, mesh=mesh, in_specs=in_specs, out_specs=out_specs, check_vma=False)
```
